32 devices in a mesh: groups: 2 (over x), adapter: 4 (over y, core), tensor: 4 (over z).
Axes of the slice: x: 2, y: 2, z: 4, core: 2. Of those that a mesh axis runs over, the one named last changes fastest.
Arguments:
- tokens: bfloat16 [4096, 8192], P(('groups', 'adapter'), 'tensor'), parts along dimension 0, may hold values from -6 to 6
- queries: bfloat16 [4096, 8192], P(('groups', 'adapter'), 'tensor'), parts along dimension 0, may hold values from -24 to 24
- kv_cache: bfloat16 [4096, 16, 2048], P(('groups', 'adapter'), None, 'tensor'), parts along dimension 0, may hold values from -24 to 24
- kv_lengths: int32 [4096], P(('groups', 'adapter')), parts along dimension 0, may hold values from 2 to 16, as said below
- variant_ids: int32 [4096, 1], P(('groups', 'adapter')), parts along dimension 0, may hold values from 0 to 7; in each aligned block of 512 rows (0 to 511, 512 to 1023, ...) at most 160 rows name the same one
- base_weight: bfloat16 [8192, 2048], P('tensor'), may hold values from -0.0625 to 0.0625
- delta_down: bfloat16 [8, 8192, 256], P('adapter', 'tensor'), may hold values from -0.0625 to 0.0625
- delta_up: bfloat16 [8, 256, 2048], P('adapter', None, 'tensor'), may hold values from -0.375 to 0.375
Outputs:
- fresh_kv: bfloat16 [4096, 2048], P(('groups', 'adapter'), 'tensor'), parts along dimension 0
- attended: bfloat16 [4096, 8192], P(('groups', 'adapter'), 'tensor'), parts along dimension 0
The draws below stay inside these ranges and needn't reach their ends.
There are 2 independent parts, one for each index of `groups`. The reference program is written for one: setup_inputs(seed, part) draws one part's arguments, and reference() takes and returns one part's arrays. A program takes and returns all parts, laid end to end along the dimension named above; an argument that names none is the same for every part. Nothing has to cross between parts.
Inputs may be any that keep to these rules, and one draw needn't show every extreme that they name: `variant_ids`: in each aligned block of 512 requests (the requests of one index of adapter) no variant appears more than 160 times, and some variant appears exactly 160 times in some block. `kv_lengths`: every request has at least two cached positions; the first request has 16.
All inputs are finite; a program needn't handle non-finite values.
Results may differ from the reference program's by a relative error of at most 0.006.
Values may be sent and summed in bfloat16 or wider, within the bound.
No kernel may reach another device: no remote copies, remote signals or barrier semaphores. Data moves between devices by JAX's collectives and lax.ppermute only.
A program may use at most 192 MiB of HBM per device.

```python
import math
import jax
import jax.numpy as jnp
import numpy as np
from jax import lax

D = 8192
HEADS = 64
KV_HEADS = 8
HEAD = 128
RANK = 256
REQ_DEV = 512
LEN = 16
VARIANTS = 8
REQUESTS = 2048
KVW = 2048
MOST = 160
N_ADAPTER = 4


def draw_queries(key, part):
    key = jax.random.fold_in(key, 1)
    result = jnp.clip(jax.random.normal(key, (REQUESTS, HEADS * HEAD), jnp.float32), -4.0, 4.0)
    return result.astype(jnp.bfloat16)


def draw_kv_cache(key, part):
    key = jax.random.fold_in(key, 2)
    result = jnp.clip(jax.random.normal(key, (REQUESTS, LEN, KV_HEADS, 2, HEAD), jnp.float32), -4.0, 4.0)
    return result.reshape(REQUESTS, LEN, KVW).astype(jnp.bfloat16)


def draw_kv_lengths(key, part):
    key = jax.random.fold_in(key, 3)
    drawn = jax.random.randint(key, (REQUESTS,), 2, LEN + 1, jnp.int32)
    return jnp.where(jnp.arange(REQUESTS, dtype=jnp.int32) == 0, jnp.int32(LEN), drawn).astype(jnp.int32)


def steps_of(key, extent, pieces, low, high):
    factor_of, own = 1.0, jax.random.fold_in(key, 6)
    for axis_at, parts in pieces:
        heights = jnp.exp(jax.random.uniform(jax.random.fold_in(own, axis_at), (parts,), jnp.float32, low / len(pieces), high / len(pieces)))
        factor_of = factor_of * jnp.repeat(heights, extent[axis_at] // parts).reshape([-1 if axis == axis_at else 1 for axis in range(len(extent))])
    return factor_of


def assign_block(rng, own, number, rows, amount, top, reach, slope):
    sequence = jax.random.permutation(rng, amount)
    crowded, ordinary = portions_of(amount, rows * top, reach, slope, True), portions_of(amount, rows * top, reach, slope, False)
    places = jnp.arange(amount)

    def named(sizes, turn):
        used = int((sizes > 0).sum())
        fixed = max(1, used // 4)
        passed = fixed + (places - fixed + turn * (used - fixed)) % max(1, amount - fixed)
        return jnp.zeros((amount,), jnp.int32).at[sequence[jnp.where(places < fixed, places, passed)]].set(jnp.asarray(sizes, jnp.int32))

    sizes = jnp.where(number % 4 == 0, named(crowded, number // 4), named(ordinary, number - number // 4 - 1))
    mixed = jax.random.permutation(jax.random.fold_in(own, 3), amount)
    giver, sink = mixed[0:amount // 2 * 2:2], mixed[1:amount // 2 * 2:2]
    slack = jnp.minimum(sizes[giver] - 1, reach - sizes[sink]) // 2
    slack = jnp.where((giver == sequence[0]) | (sink == sequence[0]) | (sizes[sink] == 0), 0, jnp.maximum(slack, 0))
    passed = jax.random.randint(jax.random.fold_in(own, 4), (amount // 2,), 0, 1 << 20) % (slack + 1)
    sizes = sizes.at[giver].add(-passed).at[sink].add(passed)
    labels = jnp.searchsorted(jnp.cumsum(sizes), jnp.arange(rows * top), side="right").astype(jnp.int32)
    table = labels.reshape(top, rows).T
    table = table[jax.random.permutation(jax.random.fold_in(own, 1), rows)]
    turn = jax.random.randint(jax.random.fold_in(own, 2), (rows, 1), 0, top)
    return jnp.take_along_axis(table, (jnp.arange(top)[None, :] + turn) % top, axis=1)


def portions_of(number_of, total, bound, lean, full):
    loads = [(1 << 20) // math.isqrt(standing ** lean) + 1 for standing in range(1, number_of + 1)]
    largest = bound if full else min(bound, max(-(-total // number_of), total * loads[0] // sum(loads)))
    least = 1 if total - largest >= number_of - 1 else 0
    given, rest = [largest] + [least] * (number_of - 1), total - largest - least * (number_of - 1)
    while rest > 0:
        free = [i for i in range(1, number_of) if given[i] < largest] or [i for i in range(1, number_of) if given[i] < bound]
        pool, budget = sum([loads[i] for i in free]), rest
        for i in free:
            addition = min(bound - given[i], max(1, budget * loads[i] // pool), rest)
            given[i] = given[i] + addition
            rest = rest - addition
    return np.array(given)


def bell_draw(rng, extent, width, bound, pieces=(), held_as=jnp.bfloat16):
    values = jax.random.normal(rng, extent, jnp.float32) * width
    if len(pieces) > 0:
        values = steps_of(rng, extent, pieces, -0.22, 0.18) * values
    return jnp.clip(values, min=-bound, max=bound).astype(held_as)


def setup_inputs(seed: int = 0, part: int = 0) -> dict:
    arg_keys = jax.random.split(jax.random.key(seed), 9)
    own_keys = jax.random.split(jax.random.fold_in(arg_keys[8], part), 9)
    tokens = bell_draw(own_keys[0], (REQUESTS, D), 1.0, 6.0, ((0, 4), (1, 4)))
    queries = draw_queries(jax.random.fold_in(jax.random.fold_in(arg_keys[8], part), 71), part)
    kv_cache = draw_kv_cache(jax.random.fold_in(jax.random.fold_in(arg_keys[8], part), 71), part)
    kv_lengths = draw_kv_lengths(jax.random.fold_in(jax.random.fold_in(arg_keys[8], part), 71), part)
    variant_ids_keys = jax.random.split(jax.random.fold_in(own_keys[4], 1), REQUESTS // REQ_DEV)
    variant_ids_turns = jax.random.permutation(jax.random.fold_in(own_keys[4], 3), REQUESTS // REQ_DEV)
    variant_ids = jax.vmap(lambda own, number: assign_block(jax.random.fold_in(own_keys[4], 2), own, number, REQ_DEV, VARIANTS, 1, MOST, 1))(variant_ids_keys, variant_ids_turns).reshape((REQUESTS, 1))
    base_weight = bell_draw(arg_keys[5], (D, KVW), D ** -0.5, 0.0625, ((0, 4),))
    delta_down = bell_draw(arg_keys[6], (VARIANTS, D, RANK), D ** -0.5, 0.0625, ((0, 4), (1, 4)))
    delta_up = bell_draw(arg_keys[7], (VARIANTS, RANK, KVW), RANK ** -0.5, 0.375, ((0, 4), (2, 4)))
    return {"tokens": tokens, "queries": queries, "kv_cache": kv_cache, "kv_lengths": kv_lengths, "variant_ids": variant_ids, "base_weight": base_weight, "delta_down": delta_down, "delta_up": delta_up}


def slot_table(variant_list, variant_count, capacity):
    row_count = variant_list.shape[0]
    one_hot = (variant_list[:, None] == jnp.arange(variant_count, dtype=jnp.int32)[None, :]).astype(jnp.int32)
    ranking = jnp.cumsum(one_hot, axis=0)
    slot_in = jnp.sum(ranking * one_hot, axis=1) - 1
    flat_slot = (variant_list * capacity + slot_in).astype(jnp.int32)
    row_of = jnp.full((variant_count * capacity,), row_count, jnp.int32)
    row_of = row_of.at[flat_slot].set(jnp.arange(row_count, dtype=jnp.int32))
    return flat_slot, row_of


def reference(tokens, queries, kv_cache, kv_lengths, variant_ids, base_weight, delta_down, delta_up):
    base_part = jnp.dot(tokens, base_weight, preferred_element_type=jnp.float32)
    down_wide = delta_down.astype(jnp.float32)
    up_wide = delta_up.astype(jnp.float32)
    token_blocks = tokens.reshape(N_ADAPTER, REQ_DEV, D)
    id_blocks = variant_ids[:, 0].reshape(N_ADAPTER, REQ_DEV)

    def one_block(packed):
        block_rows, block_ids = packed
        flat_slot, row_of = slot_table(block_ids, VARIANTS, MOST)
        padded = jnp.concatenate([block_rows, jnp.zeros((1, D), jnp.bfloat16)], axis=0)
        slotted = padded[row_of].reshape(VARIANTS, MOST, D)
        lowrank = jnp.einsum("vmd,vdr->vmr", slotted.astype(jnp.float32), down_wide).astype(jnp.bfloat16)
        change = jnp.einsum("vmr,vrc->vmc", lowrank.astype(jnp.float32), up_wide).astype(jnp.bfloat16)
        return change.reshape(VARIANTS * MOST, KVW)[flat_slot]

    delta_rows = lax.map(one_block, (token_blocks, id_blocks)).reshape(REQUESTS, KVW)
    fresh_kv = (base_part + delta_rows.astype(jnp.float32)).astype(jnp.bfloat16)

    group = HEADS // KV_HEADS
    query_four = queries.reshape(REQUESTS, KV_HEADS, group, HEAD).astype(jnp.float32)
    cache_five = kv_cache.reshape(REQUESTS, LEN, KV_HEADS, 2, HEAD).astype(jnp.float32)
    fresh_four = fresh_kv.reshape(REQUESTS, KV_HEADS, 2, HEAD).astype(jnp.float32)
    score_scale = HEAD ** -0.5
    scores = jnp.einsum("rgqd,rpgd->rgqp", query_four, cache_five[:, :, :, 0]) * score_scale
    own_score = jnp.einsum("rgqd,rgd->rgq", query_four, fresh_four[:, :, 0]) * score_scale
    visible = (jnp.arange(LEN, dtype=jnp.int32)[None, :] < kv_lengths[:, None])[:, None, None, :]
    scores = jnp.where(visible, scores, jnp.float32(-1e30))
    largest = jnp.maximum(jnp.max(scores, axis=-1), own_score)
    weights = jnp.where(visible, jnp.exp(scores - largest[..., None]), jnp.float32(0.0))
    own_weight = jnp.exp(own_score - largest)
    denominator = jnp.sum(weights, axis=-1) + own_weight
    probs = (weights / denominator[..., None]).astype(jnp.bfloat16)
    own_prob = (own_weight / denominator).astype(jnp.bfloat16)
    mixed = jnp.einsum("rgqp,rpgd->rgqd", probs.astype(jnp.float32), cache_five[:, :, :, 1])
    mixed = mixed + own_prob.astype(jnp.float32)[..., None] * fresh_four[:, :, None, 1]
    attended = mixed.astype(jnp.bfloat16).reshape(REQUESTS, HEADS * HEAD)
    return fresh_kv, attended
```

```python
import functools

import jax
import jax.numpy as jnp
from jax import lax
from jax.experimental import pallas as pl
from jax.experimental.pallas import tpu as pltpu
from jax.sharding import PartitionSpec as P

HEAD = 128
BF16 = jnp.bfloat16
F32 = jnp.float32


def params(mib):
    return pltpu.CompilerParams(vmem_limit_bytes=mib << 20)


def cost(flops, bytes_accessed):
    return pl.CostEstimate(flops=flops, bytes_accessed=bytes_accessed, transcendentals=0)


def swap(value, axis, bit):
    return lax.ppermute(value, axis, [(i, i ^ bit) for i in range(lax.axis_size(axis))])


def project_kernel(count, steps, shards_ref, x_ref, w_ref, *outs):
    del shards_ref
    step = pl.program_id(0)
    result = jnp.dot(x_ref[...], w_ref[...], preferred_element_type=F32).astype(BF16)
    for i in range(count):

        @pl.when(step // steps == i)
        def _(i=i):
            outs[i][...] = result


def project(tokens, weight, shards, width):
    rows, depth = tokens.shape
    count = len(shards)
    block = min(width, 256)
    steps = width // block

    def out_map(i, step, shards_ref):
        return (0, jnp.clip(step - i * steps, 0, steps - 1))

    return pl.pallas_call(
        functools.partial(project_kernel, count, steps),
        out_shape=[jax.ShapeDtypeStruct((rows, width), BF16)] * count,
        grid_spec=pltpu.PrefetchScalarGridSpec(
            num_scalar_prefetch=1,
            grid=(count * steps,),
            in_specs=[
                pl.BlockSpec((rows, depth), lambda step, shards_ref: (0, 0)),
                pl.BlockSpec(
                    (depth, block),
                    lambda step, shards_ref: (0, shards_ref[step // steps] * steps + step % steps),
                ),
            ],
            out_specs=[
                pl.BlockSpec((rows, block), functools.partial(out_map, i)) for i in range(count)
            ],
        ),
        compiler_params=params(40),
        cost_estimate=cost(
            2 * rows * depth * width * count, 2 * (rows * depth + (rows + depth) * width * count)
        ),
        name="project",
    )(jnp.stack(shards).astype(jnp.int32), tokens, weight)


def codes_kernel(sizes, steps, has_start, ids_ref, variant_ref, x_ref, *refs):
    weights = refs[: len(sizes)]
    start_ref = refs[len(sizes)] if has_start else None
    out_ref, total = refs[-2:]
    step = pl.program_id(0)
    width = out_ref.shape[1]
    x = x_ref[...]

    @pl.when(step == 0)
    def _():
        total[...] = jnp.zeros_like(total)

    flat = [w.at[j] for w, size in zip(weights, sizes) for j in range(size)]
    pair = max(1, 256 // width)
    for first in range(0, len(flat), pair):
        group = flat[first : first + pair]
        w = jnp.concatenate([g[...] for g in group], axis=1)
        columns = pl.ds(first * width, len(group) * width)
        total[:, columns] += jnp.dot(x, w, preferred_element_type=F32)

    @pl.when(step == steps - 1)
    def _():
        kept = start_ref[...] if has_start else jnp.zeros(out_ref.shape, F32)
        for i in range(len(flat)):
            mine = variant_ref[...] == ids_ref[i]
            kept = jnp.where(mine, total[:, i * width : (i + 1) * width], kept)
        out_ref[...] = kept.astype(out_ref.dtype)


def codes(tokens, variant_ids, weights, ids, start, start_at, dtype):
    rows, depth = tokens.shape
    width = weights[0].shape[2]
    sizes = [w.shape[0] for w in weights]
    block = min(depth, 512)
    steps = depth // block
    operands = [variant_ids, tokens] + list(weights)
    in_specs = [
        pl.BlockSpec((rows, 1), lambda k, ids_ref: (0, 0)),
        pl.BlockSpec((rows, block), lambda k, ids_ref: (0, k)),
    ] + [pl.BlockSpec((m, block, width), lambda k, ids_ref: (0, k, 0)) for m in sizes]
    if start is not None:
        operands.append(start)
        in_specs.append(pl.BlockSpec((rows, width), lambda k, ids_ref: (0, start_at)))
    return pl.pallas_call(
        functools.partial(codes_kernel, sizes, steps, start is not None),
        out_shape=jax.ShapeDtypeStruct((rows, width), dtype),
        grid_spec=pltpu.PrefetchScalarGridSpec(
            num_scalar_prefetch=1,
            grid=(steps,),
            in_specs=in_specs,
            out_specs=pl.BlockSpec((rows, width), lambda k, ids_ref: (0, 0)),
            scratch_shapes=[pltpu.VMEM((rows, sum(sizes) * width), F32)],
        ),
        compiler_params=params(48),
        cost_estimate=cost(
            2 * rows * depth * width * sum(sizes), 2 * depth * (rows + width * sum(sizes))
        ),
        name="codes",
    )(ids, *operands)


def cached_kernel(positions, group, len_ref, q_ref, kv_ref, out_ref, lse_ref):
    rows = q_ref.shape[0]
    kv_local = kv_ref.shape[2] // (2 * HEAD)
    scale = HEAD ** (-0.5)
    near = 128 // positions
    lane = lax.broadcasted_iota(jnp.int32, (near, 128), 1)
    sublane = lax.broadcasted_iota(jnp.int32, (near, 128), 0)
    same = lane // positions == sublane
    at = lane % positions
    ones = jnp.ones((128, HEAD), BF16)

    for base in range(0, rows, 2 * near):
        here = pl.ds(base, 2 * near)
        seen = [same & (at < len_ref[pl.ds(base + half * near, near), :]) for half in range(2)]
        table = [jnp.zeros((near, 128), F32) for _ in range(2)]
        for g in range(kv_local):
            at_key, at_value = 2 * g * HEAD, (2 * g + 1) * HEAD
            keys = kv_ref[here, :, at_key : at_key + HEAD].reshape(256, HEAD)
            values = kv_ref[here, :, at_value : at_value + HEAD].reshape(256, HEAD)
            query = jnp.concatenate(
                [
                    q_ref[here, (g * group + h) * HEAD : (g * group + h + 1) * HEAD]
                    for h in range(group)
                ],
                axis=0,
            )
            scores = lax.dot_general(
                query, keys, (((1,), (1,)), ((), ())), preferred_element_type=F32
            ).reshape(group, 2, near, 256)
            results = []
            for half in range(2):
                own = scores[:, half, :, half * 128 : (half + 1) * 128] * scale
                own = jnp.where(seen[half][None], own, jnp.float32(-1e30))
                largest = jnp.max(own, axis=-1, keepdims=True)
                weight = jnp.exp(own - largest).astype(BF16).reshape(group * near, 128)
                value = jnp.concatenate([values[half * 128 : (half + 1) * 128], ones], axis=1)
                mixed = jnp.dot(weight, value, preferred_element_type=F32)
                total = mixed[:, HEAD:]
                results.append((mixed[:, :HEAD] / total).reshape(group, near, HEAD))
                lse = largest + jnp.log(total).reshape(group, near, 128)
                for h in range(group):
                    table[half] = jnp.where(lane == g * group + h, lse[h], table[half])
            both = jnp.stack(results, axis=1).reshape(group, 2 * near, HEAD).astype(BF16)
            for h in range(group):
                out_ref[here, (g * group + h) * HEAD : (g * group + h + 1) * HEAD] = both[h]
        for half in range(2):
            lse_ref[pl.ds(base + half * near, near), :] = table[half]


def cached(queries, kv_cache, lengths):
    rows, features = queries.shape
    positions, width = kv_cache.shape[1:]
    group = features * 2 // width
    block = 64
    return pl.pallas_call(
        functools.partial(cached_kernel, positions, group),
        out_shape=[
            jax.ShapeDtypeStruct((rows, features), BF16),
            jax.ShapeDtypeStruct((rows, 128), F32),
        ],
        grid=(rows // block,),
        in_specs=[
            pl.BlockSpec((block, 1), lambda i: (i, 0)),
            pl.BlockSpec((block, features), lambda i: (i, 0)),
            pl.BlockSpec((block, positions, width), lambda i: (i, 0, 0)),
        ],
        out_specs=[
            pl.BlockSpec((block, features), lambda i: (i, 0)),
            pl.BlockSpec((block, 128), lambda i: (i, 0)),
        ],
        compiler_params=params(40),
        cost_estimate=cost(
            2 * rows * features * 1024, 2 * rows * (2 * features + positions * width)
        ),
        name="cached",
    )(lengths, queries, kv_cache)


def finish_kernel(counts, group, ids_ref, variant_ref, q_ref, out1_ref, lse_ref, *refs):
    terms, codes_a, codes_b, ups = counts
    refs = list(refs)
    take = lambda n: [refs.pop(0) for _ in range(n)]
    base_refs, a_refs, b_refs, up_refs = take(terms), take(codes_a), take(codes_b), take(len(ups))
    fresh_ref, attended_ref = refs
    variant = variant_ref[...]

    def total(parts):
        result = parts[0][...].astype(F32)
        for part in parts[1:]:
            result = result + part[...].astype(F32)
        return result

    code = jnp.concatenate([total(a_refs).astype(BF16), total(b_refs).astype(BF16)], axis=1)
    change = jnp.zeros(fresh_ref.shape, F32)
    at = 0
    for up_ref, size in zip(up_refs, ups):
        for j in range(size):
            mine = jnp.where(variant == ids_ref[at], code, jnp.zeros_like(code))
            change = change + jnp.dot(mine, up_ref[j], preferred_element_type=F32)
            at += 1
    fresh = (total(base_refs) + change.astype(BF16).astype(F32)).astype(BF16)
    fresh_ref[...] = fresh
    ones = jnp.ones((2 * HEAD, HEAD), BF16)
    scale = HEAD ** (-0.5)
    for g in range(fresh.shape[1] // (2 * HEAD)):
        key = fresh[:, 2 * g * HEAD : (2 * g + 1) * HEAD].astype(F32)
        value = fresh[:, (2 * g + 1) * HEAD : (2 * g + 2) * HEAD].astype(F32)
        for h in range(g * group, (g + 1) * group):
            columns = slice(h * HEAD, (h + 1) * HEAD)
            product = q_ref[:, columns].astype(F32) * key
            high = product.astype(BF16)
            low = (product - high.astype(F32)).astype(BF16)
            score = jnp.dot(
                jnp.concatenate([high, low], axis=1), ones, preferred_element_type=F32
            )
            weight = 1.0 / (1.0 + jnp.exp(lse_ref[:, h : h + 1] - score * scale))
            old = out1_ref[:, columns].astype(F32)
            attended_ref[:, columns] = (old + weight * (value - old)).astype(BF16)


def finish(variant_ids, queries, out1, lse, base_terms, codes_a, codes_b, ups, ids):
    rows, features = queries.shape
    width = base_terms[0].shape[1]
    rank_part = codes_a[0].shape[1]
    group = features * 2 // width
    block = 128
    by_row = lambda columns: pl.BlockSpec((block, columns), lambda i, ids_ref: (i, 0))
    counts = (len(base_terms), len(codes_a), len(codes_b), [u.shape[0] for u in ups])
    return pl.pallas_call(
        functools.partial(finish_kernel, counts, group),
        out_shape=[
            jax.ShapeDtypeStruct((rows, width), BF16),
            jax.ShapeDtypeStruct((rows, features), BF16),
        ],
        grid_spec=pltpu.PrefetchScalarGridSpec(
            num_scalar_prefetch=1,
            grid=(rows // block,),
            in_specs=[by_row(1), by_row(features), by_row(features), by_row(128)]
            + [by_row(width)] * len(base_terms)
            + [by_row(rank_part)] * (len(codes_a) + len(codes_b))
            + [pl.BlockSpec(u.shape, lambda i, ids_ref: (0, 0, 0)) for u in ups],
            out_specs=[by_row(width), by_row(features)],
        ),
        compiler_params=params(40),
        cost_estimate=cost(
            2 * rows * width * 256 * sum(counts[3]), 2 * rows * (3 * features + 4 * width)
        ),
        name="finish",
    )(ids, variant_ids, queries, out1, lse, *base_terms, *codes_a, *codes_b, *ups)


def reduce_base(tokens, weight, width):
    size = lax.axis_size("tensor")
    me = lax.axis_index("tensor")
    last = size - 1
    parts = {last: [project(tokens, weight, [me ^ last], width)[0]]}
    others = [t for t in range(last - 1, -1, -1)]
    others.sort(key=lambda t: -(t & 1))
    for t, part in zip(others, project(tokens, weight, [me ^ t for t in others], width)):
        parts[t] = [part]
    bit = 1
    while bit < size:
        for t in range(last, 0, -1):
            if t & bit and t & (bit - 1) == 0:
                total = parts[t][0]
                if len(parts[t]) > 1:
                    total = sum(part.astype(F32) for part in parts[t]).astype(BF16)
                parts[t ^ bit].append(swap(total, "tensor", bit))
        bit *= 2
    return parts[0]


def all_reduce(value):
    size = lax.axis_size("tensor")
    bit = 1
    terms = [value]
    while bit < size:
        if len(terms) > 1:
            terms = [sum(term.astype(F32) for term in terms).astype(BF16)]
        terms.append(swap(terms[0], "tensor", bit))
        bit *= 2
    return terms


def low_rank(tokens, variant_ids, delta_down, delta_up):
    owners = lax.axis_size("adapter")
    mine = lax.axis_index("adapter")
    local, depth, rank = delta_down.shape
    half = rank // 2
    down = [delta_down[:, :, :half], delta_down[:, :, half:]]
    if owners != 4 or lax.axis_size("groups") != 2 or local != 2:
        ids = jnp.arange(owners * local, dtype=jnp.int32)
        every = lax.all_gather(delta_down, "adapter", axis=0, tiled=True)
        up = lax.all_gather(delta_up, "adapter", axis=0, tiled=True)
        both = [
            codes(tokens, variant_ids, [every[:, :, at : at + half]], ids, None, 0, BF16)
            for at in (0, half)
        ]
        return both, [up], ids
    group = lax.axis_index("groups")
    first = lax.dynamic_slice_in_dim(down[0], group, 1, axis=0)
    from_y = swap(first, "adapter", 2)
    near = swap(delta_down, "adapter", 1)
    from_x = swap(from_y, "groups", 1)
    far = swap(down[1], "adapter", 2)
    up_y = swap(delta_up, "adapter", 2)

    ids_near = [2 * mine, 2 * mine + 1, 2 * (mine ^ 1), 2 * (mine ^ 1) + 1]
    start = codes(
        tokens, variant_ids, [delta_down, near], jnp.stack(ids_near), None, 0, F32
    )
    pair_a = jnp.concatenate([from_y, from_x], axis=0)
    pair_a_near = swap(pair_a, "adapter", 1)
    lane, lane_near = 2 * (mine ^ 2), 2 * (mine ^ 3)
    ids_a = [lane + group, lane + 1 - group, lane_near + group, lane_near + 1 - group]
    part_a = codes(
        tokens, variant_ids, [pair_a, pair_a_near], jnp.stack(ids_a), start, 0, BF16
    )
    far_near = swap(far, "adapter", 1)
    ids_b = [lane, lane + 1, lane_near, lane_near + 1]
    part_b = codes(
        tokens, variant_ids, [far, far_near], jnp.stack(ids_b), start, 1, BF16
    )
    up_two = jnp.concatenate([delta_up, up_y], axis=0)
    up_near = swap(up_two, "adapter", 1)
    ids_up = [2 * (mine ^ k) + j for k in (0, 2, 1, 3) for j in (0, 1)]
    return [part_a, part_b], [up_two, up_near], jnp.stack(ids_up).astype(jnp.int32)


def local(tokens, queries, kv_cache, kv_lengths, variant_ids, base_weight, delta_down, delta_up):
    width = base_weight.shape[1] // lax.axis_size("tensor")
    parts, ups, ids = low_rank(tokens, variant_ids, delta_down, delta_up)
    base_terms = reduce_base(tokens, base_weight, width)
    codes_a, codes_b = [all_reduce(part) for part in parts]
    out1, lse = cached(queries, kv_cache, kv_lengths[:, None])
    fresh, attended = finish(
        variant_ids, queries, out1, lse, base_terms, codes_a, codes_b, ups, ids
    )
    return (fresh, attended)


def solution(mesh):
    return jax.shard_map(
        local,
        mesh=mesh,
        in_specs=(
            P(("groups", "adapter"), "tensor"),
            P(("groups", "adapter"), "tensor"),
            P(("groups", "adapter"), None, "tensor"),
            P(("groups", "adapter")),
            P(("groups", "adapter"), None),
            P("tensor", None),
            P("adapter", "tensor", None),
            P("adapter", None, "tensor"),
        ),
        out_specs=(P(("groups", "adapter"), "tensor"), P(("groups", "adapter"), "tensor")),
        check_vma=False,
    )
```

```python
import functools

import jax
import jax.numpy as jnp
from jax import lax
from jax.experimental import pallas as pl
from jax.experimental.pallas import tpu as pltpu
from jax.sharding import PartitionSpec as P

HEAD = 128
BF16 = jnp.bfloat16
F32 = jnp.float32
ANY = pl.BlockSpec(memory_space=pl.ANY)
WHOLE = pl.BlockSpec(memory_space=pltpu.VMEM)
SCALARS = pl.BlockSpec(memory_space=pltpu.SMEM)


def params(mib):
    return pltpu.CompilerParams(vmem_limit_bytes=mib << 20)


def brief():
    return pl.CostEstimate(flops=1, bytes_accessed=1, transcendentals=0)


def gate(value, after):
    def body(*refs):
        del refs

    return pl.pallas_call(
        body,
        out_shape=jax.ShapeDtypeStruct(value.shape, value.dtype),
        in_specs=[ANY] * (1 + len(after)),
        out_specs=ANY,
        input_output_aliases={0: 0},
        compiler_params=params(16),
        cost_estimate=brief(),
        name="gate",
    )(value, *after)


def cut(value, first, count, column, width, after):
    depth = value.shape[1]
    pieces = 2
    block = depth // pieces

    def body(first_ref, value_ref, *refs):
        out_ref, held, sems = refs[-3:]
        where = [(i, pl.ds(k * block, block), k) for i in range(count) for k in range(pieces)]
        loads = [
            pltpu.make_async_copy(
                value_ref.at[first_ref[0] + i, rows, pl.ds(column * width, width)],
                held.at[i, rows],
                sems.at[0, i, k],
            )
            for i, rows, k in where
        ]
        stores = [
            pltpu.make_async_copy(held.at[i, rows], out_ref.at[i, rows], sems.at[1, i, k])
            for i, rows, k in where
        ]
        for load in loads:
            load.start()
        for load, store in zip(loads, stores):
            load.wait()
            store.start()
        for store in stores:
            store.wait()

    return pl.pallas_call(
        body,
        out_shape=jax.ShapeDtypeStruct((count, depth, width), value.dtype),
        in_specs=[SCALARS] + [ANY] * (1 + len(after)),
        out_specs=ANY,
        scratch_shapes=[
            pltpu.VMEM((count, depth, width), value.dtype),
            pltpu.SemaphoreType.DMA((2, count, pieces)),
        ],
        compiler_params=params(16),
        cost_estimate=brief(),
        name="cut",
    )(jnp.full((1,), first, jnp.int32), value, *after)


def permute(value, axis, pairs):
    return lax.ppermute(value, axis, pairs)


def swap(value, axis, bit):
    return lax.ppermute(value, axis, [(i, i ^ bit) for i in range(lax.axis_size(axis))])


def added(terms):
    return sum(term.astype(F32) for term in terms).astype(BF16)


def project(tokens, weight, shards, width, after):
    rows, depth = tokens.shape
    count = len(shards)
    pieces = 4
    block = depth // pieces

    def body(shards_ref, x_ref, w_ref, *refs):
        outs = refs[len(after) : len(after) + count]
        held, made, load_sems, store_sems = refs[len(after) + count :]
        loads = [
            [
                pltpu.make_async_copy(
                    w_ref.at[
                        pl.ds(k * block, block),
                        pl.ds(pl.multiple_of(shards_ref[i] * width, width), width),
                    ],
                    held.at[i, pl.ds(k * block, block)],
                    load_sems.at[i, k],
                )
                for k in range(pieces)
            ]
            for i in range(count)
        ]
        stores = [
            pltpu.make_async_copy(made.at[i], outs[i], store_sems.at[i]) for i in range(count)
        ]
        for group in loads:
            for load in group:
                load.start()
        for i in range(count):
            if i == 0:
                total = jnp.zeros((rows, width), F32)
                for k in range(pieces):
                    loads[0][k].wait()
                    part = slice(k * block, (k + 1) * block)
                    total = total + jnp.dot(
                        x_ref[:, part], held[0, part], preferred_element_type=F32
                    )
                made[0] = total.astype(BF16)
            else:
                for k in range(pieces):
                    loads[i][k].wait()
                made[i] = jnp.dot(x_ref[...], held[i], preferred_element_type=F32).astype(BF16)
            stores[i].start()
        for store in stores:
            store.wait()

    return pl.pallas_call(
        body,
        out_shape=[jax.ShapeDtypeStruct((rows, width), BF16)] * count,
        in_specs=[SCALARS, WHOLE] + [ANY] * (1 + len(after)),
        out_specs=[ANY] * count,
        scratch_shapes=[
            pltpu.VMEM((count, depth, width), BF16),
            pltpu.VMEM((count, rows, width), BF16),
            pltpu.SemaphoreType.DMA((count, pieces)),
            pltpu.SemaphoreType.DMA((count,)),
        ],
        compiler_params=params(48),
        cost_estimate=brief(),
        name="project",
    )(jnp.stack(shards).astype(jnp.int32), tokens, weight, *after)


def codes(sets, weights, ids, column, dtypes, after):
    depth, width = weights[0].shape[1:]
    sizes = [w.shape[0] for w in weights]
    has_start = [start is not None for _, _, start in sets]
    chunk = 256
    pair = max(1, 256 // width)

    def body(ids_ref, *refs):
        refs = list(refs)
        inputs = []
        for started in has_start:
            inputs.append([refs.pop(0) for _ in range(3 if started else 2)])
        flat = [w.at[j] for w, size in zip(refs[: len(sizes)], sizes) for j in range(size)]
        outs = refs[-len(sets) :]
        groups = [flat[at : at + pair] for at in range(0, len(flat), pair)]
        for out_ref, given in zip(outs, inputs):
            for row in range(0, out_ref.shape[0], chunk):
                here = slice(row, row + chunk)
                x, variant = given[0][here], given[1][here]
                if len(given) == 3:
                    kept = given[2][here, column : column + width]
                else:
                    kept = jnp.zeros((x.shape[0], width), F32)
                for g, group in enumerate(groups):
                    w = jnp.concatenate([entry[...] for entry in group], axis=1)
                    product = jnp.dot(x, w, preferred_element_type=F32)
                    for j in range(len(group)):
                        mine = variant == ids_ref[g * pair + j]
                        kept = jnp.where(mine, product[:, j * width : (j + 1) * width], kept)
                out_ref[here] = kept.astype(out_ref.dtype)

    operands = []
    for tokens, variant, start in sets:
        operands += [tokens, variant] + ([start] if start is not None else [])
    return pl.pallas_call(
        body,
        out_shape=[
            jax.ShapeDtypeStruct((tokens.shape[0], width), dtype)
            for (tokens, _, _), dtype in zip(sets, dtypes)
        ],
        in_specs=[SCALARS] + [WHOLE] * (len(operands) + len(weights)) + [ANY] * len(after),
        out_specs=[WHOLE] * len(sets),
        compiler_params=params(30),
        cost_estimate=brief(),
        name="codes",
    )(ids.astype(jnp.int32), *operands, *weights, *after)


def cached_kernel(positions, group, len_ref, q_ref, kv_ref, *refs):
    out_ref, lse_ref = refs[-2:]
    rows = q_ref.shape[0]
    kv_local = kv_ref.shape[2] // (2 * HEAD)
    scale = HEAD ** (-0.5)
    near = 128 // positions
    lane = lax.broadcasted_iota(jnp.int32, (near, 128), 1)
    sublane = lax.broadcasted_iota(jnp.int32, (near, 128), 0)
    same = lane // positions == sublane
    at = lane % positions
    ones = jnp.ones((128, HEAD), BF16)

    for base in range(0, rows, 2 * near):
        here = pl.ds(base, 2 * near)
        seen = [same & (at < len_ref[pl.ds(base + half * near, near), :]) for half in range(2)]
        table = [jnp.zeros((near, 128), F32) for _ in range(2)]
        for g in range(kv_local):
            at_key, at_value = 2 * g * HEAD, (2 * g + 1) * HEAD
            keys = kv_ref[here, :, at_key : at_key + HEAD].reshape(256, HEAD)
            values = kv_ref[here, :, at_value : at_value + HEAD].reshape(256, HEAD)
            query = jnp.concatenate(
                [
                    q_ref[here, (g * group + h) * HEAD : (g * group + h + 1) * HEAD]
                    for h in range(group)
                ],
                axis=0,
            )
            scores = lax.dot_general(
                query, keys, (((1,), (1,)), ((), ())), preferred_element_type=F32
            ).reshape(group, 2, near, 256)
            results = []
            for half in range(2):
                own = scores[:, half, :, half * 128 : (half + 1) * 128] * scale
                own = jnp.where(seen[half][None], own, jnp.float32(-1e30))
                largest = jnp.max(own, axis=-1, keepdims=True)
                weight = jnp.exp(own - largest).astype(BF16).reshape(group * near, 128)
                value = jnp.concatenate([values[half * 128 : (half + 1) * 128], ones], axis=1)
                mixed = jnp.dot(weight, value, preferred_element_type=F32)
                total = mixed[:, HEAD:]
                results.append((mixed[:, :HEAD] / total).reshape(group, near, HEAD))
                lse = largest + jnp.log(total).reshape(group, near, 128)
                for h in range(group):
                    table[half] = jnp.where(lane == g * group + h, lse[h], table[half])
            both = jnp.stack(results, axis=1).reshape(group, 2 * near, HEAD).astype(BF16)
            for h in range(group):
                out_ref[here, (g * group + h) * HEAD : (g * group + h + 1) * HEAD] = both[h]
        for half in range(2):
            lse_ref[pl.ds(base + half * near, near), :] = table[half]


def cached(queries, kv_cache, lengths, first, count, earlier, after):
    rows, features = queries.shape
    positions, width = kv_cache.shape[1:]
    group = features * 2 // width
    block = 64
    base = first // block
    return pl.pallas_call(
        functools.partial(cached_kernel, positions, group),
        out_shape=[
            jax.ShapeDtypeStruct((rows, features), BF16),
            jax.ShapeDtypeStruct((rows, 128), F32),
        ],
        grid=(count // block,),
        in_specs=[
            pl.BlockSpec((block, 1), lambda i: (base + i, 0)),
            pl.BlockSpec((block, features), lambda i: (base + i, 0)),
            pl.BlockSpec((block, positions, width), lambda i: (base + i, 0, 0)),
        ]
        + [ANY] * (len(earlier) + len(after)),
        out_specs=[
            pl.BlockSpec((block, features), lambda i: (base + i, 0)),
            pl.BlockSpec((block, 128), lambda i: (base + i, 0)),
        ],
        input_output_aliases={3 + i: i for i in range(len(earlier))},
        compiler_params=params(30),
        cost_estimate=brief(),
        name="cached",
    )(lengths, queries, kv_cache, *earlier, *after)


def finish(variant_ids, queries, out1, lse, base_terms, choice, codes_a, codes_b, ups, ids):
    rows, features = queries.shape
    width = base_terms[0].shape[1]
    group = features * 2 // width
    chunk = 128
    scale = HEAD ** (-0.5)
    flag, extra = choice
    counts = [len(base_terms), len(extra), len(codes_a), len(codes_b), len(ups)]

    def body(ids_ref, flag_ref, variant_ref, q_ref, out1_ref, lse_ref, *refs):
        refs = list(refs)
        take = lambda n: [refs.pop(0) for _ in range(n)]
        base_refs, extra_refs, a_refs, b_refs, up_refs = [take(n) for n in counts]
        fresh_ref, attended_ref, fresh_made, attended_made, sems = refs
        ones = jnp.ones((2 * HEAD, HEAD), BF16)

        def total(parts, here):
            result = parts[0][here].astype(F32)
            for part in parts[1:]:
                result = result + part[here].astype(F32)
            return result

        stores = []
        for at in range(0, rows, chunk):
            here = slice(at, at + chunk)
            variant = variant_ref[here]
            code = jnp.concatenate(
                [total(a_refs, here).astype(BF16), total(b_refs, here).astype(BF16)], axis=1
            )
            change = jnp.zeros((chunk, width), F32)
            entry = 0
            for up_ref in up_refs:
                for j in range(up_ref.shape[0]):
                    mine = jnp.where(variant == ids_ref[entry], code, jnp.zeros_like(code))
                    change = change + jnp.dot(mine, up_ref[j], preferred_element_type=F32)
                    entry += 1
            base = total(base_refs, here)
            for part in extra_refs:
                base = base + jnp.where(flag_ref[0] == 1, part[here].astype(F32), 0.0)
            fresh = (base + change.astype(BF16).astype(F32)).astype(BF16)
            fresh_made[here] = fresh
            for g in range(width // (2 * HEAD)):
                key = fresh[:, 2 * g * HEAD : (2 * g + 1) * HEAD].astype(F32)
                value = fresh[:, (2 * g + 1) * HEAD : (2 * g + 2) * HEAD].astype(F32)
                for h in range(g * group, (g + 1) * group):
                    columns = slice(h * HEAD, (h + 1) * HEAD)
                    product = q_ref[here, columns].astype(F32) * key
                    high = product.astype(BF16)
                    low = (product - high.astype(F32)).astype(BF16)
                    score = jnp.dot(
                        jnp.concatenate([high, low], axis=1), ones, preferred_element_type=F32
                    )
                    weight = 1.0 / (1.0 + jnp.exp(lse_ref[here, h : h + 1] - score * scale))
                    old = out1_ref[here, columns].astype(F32)
                    attended_made[here, columns] = (old + weight * (value - old)).astype(BF16)
            for k, (made, ref) in enumerate(
                ((fresh_made, fresh_ref), (attended_made, attended_ref))
            ):
                lines = pl.ds(at, chunk)
                stores.append(
                    pltpu.make_async_copy(made.at[lines], ref.at[lines], sems.at[k, at // chunk])
                )
                stores[-1].start()
        for store in stores:
            store.wait()

    operands = [variant_ids, queries, out1, lse, *base_terms, *extra, *codes_a, *codes_b, *ups]
    return pl.pallas_call(
        body,
        out_shape=[
            jax.ShapeDtypeStruct((rows, width), BF16),
            jax.ShapeDtypeStruct((rows, features), BF16),
        ],
        in_specs=[SCALARS, SCALARS] + [WHOLE] * len(operands),
        out_specs=[ANY, ANY],
        scratch_shapes=[
            pltpu.VMEM((rows, width), BF16),
            pltpu.VMEM((rows, features), BF16),
            pltpu.SemaphoreType.DMA((2, rows // chunk)),
        ],
        compiler_params=params(30),
        cost_estimate=brief(),
        name="finish",
    )(ids.astype(jnp.int32), jnp.full((1,), flag, jnp.int32), *operands)


def all_reduce(value):
    size = lax.axis_size("tensor")
    bit = 1
    terms = [value]
    while bit < size:
        if len(terms) > 1:
            terms = [added(terms)]
        terms.append(swap(terms[0], "tensor", bit))
        bit *= 2
    return terms


def reduce_parts(parts):
    size = lax.axis_size("tensor")
    parts = {t: [part] for t, part in parts.items()}
    bit = 1
    while bit < size:
        for t in range(size - 1, 0, -1):
            if t & bit and t & (bit - 1) == 0:
                total = parts[t][0] if len(parts[t]) == 1 else added(parts[t])
                parts[t ^ bit].append(swap(total, "tensor", bit))
        bit *= 2
    return parts[0]


def general(tokens, queries, kv_cache, lengths, variant_ids, base_weight, delta_down, delta_up):
    size, me = lax.axis_size("tensor"), lax.axis_index("tensor")
    rows = tokens.shape[0]
    width = base_weight.shape[1] // size
    owners = lax.axis_size("adapter")
    variants, _, rank = delta_down.shape
    half = rank // 2
    every = lax.all_gather(delta_down, "adapter", axis=0, tiled=True)
    up = lax.all_gather(delta_up, "adapter", axis=0, tiled=True)
    order = sorted(range(size), key=lambda t: (-(t & 1), -t))
    parts = project(tokens, base_weight, [me ^ t for t in order], width, [])
    base_terms = reduce_parts(dict(zip(order, parts)))
    ids = jnp.arange(owners * variants, dtype=jnp.int32)
    rows_of = [(tokens, variant_ids, None)]
    codes_a, codes_b = [
        all_reduce(codes(rows_of, [every[:, :, at : at + half]], ids, 0, [BF16], parts[:1])[0])
        for at in (0, half)
    ]
    out1, lse = cached(queries, kv_cache, lengths, 0, rows, [], parts[:1])
    return finish(
        variant_ids, queries, out1, lse, base_terms, (0, []), codes_a, codes_b, [up], ids
    )


def paired(tokens, queries, kv_cache, lengths, variant_ids, base_weight, delta_down, delta_up):
    me = lax.axis_index("tensor")
    mine = lax.axis_index("adapter")
    group = lax.axis_index("groups")
    rows = tokens.shape[0]
    width = base_weight.shape[1] // 4
    half = delta_down.shape[2] // 2

    first = cut(delta_down, group, 1, 0, half, [])
    from_y = swap(first, "adapter", 2)
    near = swap(tokens, "adapter", 1)
    near_ids = swap(variant_ids, "adapter", 1)
    (part_a,) = project(tokens, base_weight, [me ^ 2], width, [first])
    got_a = permute(part_a, "tensor", [(0, 1), (1, 3), (2, 0), (3, 2)])
    second = cut(delta_down, 0, 2, 1, half, [part_a])
    far = swap(second, "adapter", 2)
    part_b, part_c, own = project(
        tokens, base_weight, [me ^ 3, me ^ 1, me], width, [second]
    )
    got_b1 = permute(part_b, "tensor", [(0, 3), (3, 0)])
    got_c = swap(part_c, "tensor", 1)

    from_y = gate(from_y, [own])
    from_x = swap(from_y, "groups", 1)
    both = [(tokens, variant_ids, None), (near, near_ids, None)]
    start, start_near = codes(
        both, [delta_down], jnp.stack([2 * mine, 2 * mine + 1]), 0, [F32, F32], [own, from_y]
    )
    sum_b = added([part_b, got_a])
    got_b2 = permute(sum_b, "tensor", [(1, 2), (2, 1)])
    early = cached(queries, kv_cache, lengths, 0, rows // 2, [], [start, sum_b])
    lane = 2 * (mine ^ 2)
    both = [(tokens, variant_ids, start), (near, near_ids, start_near)]
    a, a_near = codes(
        both,
        [from_y, from_x],
        jnp.stack([lane + group, lane + 1 - group]),
        0,
        [F32, BF16],
        [early[1]],
    )
    a = added([a, swap(a_near, "adapter", 1)])
    codes_a = all_reduce(a)
    b, b_near = codes(
        both, [far], jnp.stack([lane, lane + 1]), half, [F32, BF16], [a_near]
    )
    b = added([b, swap(b_near, "adapter", 1)])
    b = gate(b, [got_b1, got_c])
    codes_b = all_reduce(b)
    up_y = swap(delta_up, "adapter", 2)
    out1, lse = cached(
        queries, kv_cache, lengths, rows // 2, rows // 2, early, [b, codes_a[0], up_y]
    )
    ups = [delta_up, up_y, swap(delta_up, "adapter", 1), swap(up_y, "adapter", 1)]
    ids = jnp.stack([2 * (mine ^ k) + j for k in (0, 2, 1, 3) for j in (0, 1)])
    ends = (me == 0) | (me == 3)
    got_b = jnp.where(ends, got_b1, got_b2)
    return finish(
        variant_ids,
        queries,
        out1,
        lse,
        [own, got_c, got_b],
        (ends.astype(jnp.int32), [got_a]),
        codes_a,
        codes_b,
        ups,
        ids,
    )


def local(tokens, queries, kv_cache, kv_lengths, variant_ids, base_weight, delta_down, delta_up):
    sizes = [lax.axis_size(axis) for axis in ("groups", "adapter", "tensor")]
    plan = paired if sizes == [2, 4, 4] and delta_down.shape[0] == 2 else general
    return tuple(
        plan(
            tokens,
            queries,
            kv_cache,
            kv_lengths[:, None],
            variant_ids,
            base_weight,
            delta_down,
            delta_up,
        )
    )


def solution(mesh):
    return jax.shard_map(
        local,
        mesh=mesh,
        in_specs=(
            P(("groups", "adapter"), "tensor"),
            P(("groups", "adapter"), "tensor"),
            P(("groups", "adapter"), None, "tensor"),
            P(("groups", "adapter")),
            P(("groups", "adapter"), None),
            P("tensor", None),
            P("adapter", "tensor", None),
            P("adapter", None, "tensor"),
        ),
        out_specs=(P(("groups", "adapter"), "tensor"), P(("groups", "adapter"), "tensor")),
        check_vma=False,
    )
```

```python
import functools

import jax
import jax.numpy as jnp
from jax import lax
from jax.experimental import pallas as pl
from jax.experimental.pallas import tpu as pltpu
from jax.sharding import PartitionSpec as P

HEAD = 128
BF16 = jnp.bfloat16
F32 = jnp.float32
ANY = pl.BlockSpec(memory_space=pl.ANY)
WHOLE = pl.BlockSpec(memory_space=pltpu.VMEM)
SCALARS = pl.BlockSpec(memory_space=pltpu.SMEM)


def params(mib):
    return pltpu.CompilerParams(vmem_limit_bytes=mib << 20)


def brief():
    return pl.CostEstimate(flops=1, bytes_accessed=1, transcendentals=0)


def gate(value, after):
    def body(*refs):
        del refs

    return pl.pallas_call(
        body,
        out_shape=jax.ShapeDtypeStruct(value.shape, value.dtype),
        in_specs=[ANY] * (1 + len(after)),
        out_specs=ANY,
        input_output_aliases={0: 0},
        compiler_params=params(16),
        cost_estimate=brief(),
        name="gate",
    )(value, *after)


def in_vmem(shape, dtype):
    return pltpu.VMEM(shape, dtype)


def in_hbm(value):
    return pltpu.with_memory_space_constraint(value, pltpu.HBM)


def cut(value, takes, after):
    depth, rank = value.shape[1:]
    half = rank // 2
    pieces = 2
    block = depth // pieces

    def body(first_ref, value_ref, *refs):
        outs, sems = refs[len(after) : -1], refs[-1]
        loads = []
        for n, (out_ref, (_, count, column)) in enumerate(zip(outs, takes)):
            for i in range(count):
                for k in range(pieces):
                    lines = pl.ds(k * block, block)
                    loads.append(
                        pltpu.make_async_copy(
                            value_ref.at[first_ref[n] + i, lines, pl.ds(column * half, half)],
                            out_ref.at[i, lines],
                            sems.at[n, i, k],
                        )
                    )
        for load in loads:
            load.start()
        for load in loads:
            load.wait()

    return pl.pallas_call(
        body,
        out_shape=[in_vmem((count, depth, half), value.dtype) for _, count, _ in takes],
        in_specs=[SCALARS] + [ANY] * (1 + len(after)),
        out_specs=[WHOLE] * len(takes),
        scratch_shapes=[
            pltpu.SemaphoreType.DMA((len(takes), max(count for _, count, _ in takes), pieces))
        ],
        compiler_params=params(16),
        cost_estimate=brief(),
        name="cut",
    )(jnp.stack([jnp.int32(first) for first, _, _ in takes]), in_hbm(value), *after)


def swap(value, axis, bit):
    return lax.ppermute(value, axis, [(i, i ^ bit) for i in range(lax.axis_size(axis))])


def added(terms):
    return sum(term.astype(F32) for term in terms).astype(BF16)


def project(tokens, weight, shards, width, after, down=None, takes=(), near_adds=()):
    rows, depth = tokens.shape
    count = len(shards)
    pieces = 4
    block = depth // pieces
    extra = 1 if takes else 0

    def body(scalars_ref, x_ref, w_ref, *refs):
        down_ref = refs[0] if extra else None
        refs = refs[extra + len(after) :]
        outs, cuts = refs[:count], refs[count : count + len(takes)]
        held, made, load_sems, store_sems = refs[count + len(takes) :][:4]
        scratch = refs[count + len(takes) + 4 :]
        loads = [
            [
                pltpu.make_async_copy(
                    w_ref.at[
                        pl.ds(k * block, block),
                        pl.ds(pl.multiple_of(scalars_ref[i] * width, width), width),
                    ],
                    held.at[i, pl.ds(k * block, block)],
                    load_sems.at[i, k],
                )
                for k in range(pieces)
            ]
            for i in range(count)
        ]
        stores = [
            pltpu.make_async_copy(made.at[i], outs[i], store_sems.at[i])
            for i in range(count)
            if i not in near_adds
        ]
        cut_in, cut_out = [], []
        for n, (_, size, column) in enumerate(takes):
            spot, sems = scratch[n], scratch[len(takes)]
            half = spot.shape[2]
            start = scalars_ref[count + n]
            cut_in.append(
                pltpu.make_async_copy(
                    down_ref.at[pl.ds(start, size), :, pl.ds(column * half, half)],
                    spot,
                    sems.at[n, 0],
                )
            )
            cut_out.append(pltpu.make_async_copy(spot, cuts[n], sems.at[n, 1]))
        for copy in cut_in[:1]:
            copy.start()
        for group in loads:
            for load in group:
                load.start()
        for copy in cut_in[1:]:
            copy.start()
        for i in range(count):
            if i == 0:
                total = jnp.zeros((rows, width), F32)
                for k in range(pieces):
                    loads[0][k].wait()
                    part = slice(k * block, (k + 1) * block)
                    total = total + jnp.dot(
                        x_ref[:, part], held[0, part], preferred_element_type=F32
                    )
                result = total.astype(BF16)
            else:
                for k in range(pieces):
                    loads[i][k].wait()
                result = jnp.dot(x_ref[...], held[i], preferred_element_type=F32).astype(BF16)
            if i in near_adds:
                outs[i][...] = result
            else:
                made[i] = result
                stores[sum(1 for n in range(i) if n not in near_adds)].start()
            if i == 0:
                for copy, out in zip(cut_in, cut_out):
                    copy.wait()
                    out.start()
        for store in stores + cut_out:
            store.wait()

    shapes = [
        (in_vmem if i in near_adds else pltpu.HBM)((rows, width), BF16) for i in range(count)
    ]
    scratch = [
        pltpu.VMEM((count, depth, width), BF16),
        pltpu.VMEM((count, rows, width), BF16),
        pltpu.SemaphoreType.DMA((count, pieces)),
        pltpu.SemaphoreType.DMA((count,)),
    ]
    operands = [tokens, in_hbm(weight)]
    scalars = list(shards)
    if extra:
        operands.append(in_hbm(down))
        for first, size, _ in takes:
            piece = (size, depth, down.shape[2] // 2)
            shapes.append(pltpu.HBM(piece, BF16))
            scratch.append(pltpu.VMEM(piece, BF16))
            scalars.append(first)
        scratch.append(pltpu.SemaphoreType.DMA((len(takes), 2)))
    return pl.pallas_call(
        body,
        out_shape=shapes,
        in_specs=[SCALARS, WHOLE] + [ANY] * (1 + extra + len(after)),
        out_specs=[WHOLE if i in near_adds else ANY for i in range(len(shapes))],
        scratch_shapes=scratch,
        compiler_params=params(20),
        cost_estimate=brief(),
        name="project",
    )(jnp.stack([jnp.int32(n) for n in scalars]), *operands, *after)


def near_codes(tokens, variant, near, near_variant, down, ids, after):
    rows, depth = tokens.shape
    count, _, rank = down.shape
    chunk = 256

    def body(ids_ref, x_ref, variant_ref, near_ref, near_variant_ref, down_ref, *refs):
        out_ref, near_out_ref, kept_ref, held, sems = refs[-5:]
        loads = [
            pltpu.make_async_copy(down_ref.at[j], held.at[j], sems.at[j]) for j in range(count)
        ]
        copy = pltpu.make_async_copy(near_ref, kept_ref, sems.at[count])
        loads[0].start()
        copy.start()
        for load in loads[1:]:
            load.start()
        for j in range(count):
            loads[j].wait()
            for source, named, result in (
                (x_ref, variant_ref, out_ref),
                (kept_ref, near_variant_ref, near_out_ref),
            ):
                if j == 0 and source is kept_ref:
                    copy.wait()
                for row in range(0, rows, chunk):
                    here = slice(row, row + chunk)
                    product = jnp.dot(source[here], held[j], preferred_element_type=F32)
                    other = result[here] if j > 0 else jnp.zeros_like(product)
                    result[here] = jnp.where(named[here] == ids_ref[j], product, other)

    return pl.pallas_call(
        body,
        out_shape=[
            in_vmem((rows, rank), F32),
            in_vmem((rows, rank), F32),
            in_vmem((rows, depth), BF16),
        ],
        in_specs=[SCALARS, WHOLE, WHOLE, ANY, WHOLE, ANY] + [ANY] * len(after),
        out_specs=[WHOLE] * 3,
        scratch_shapes=[
            pltpu.VMEM(down.shape, BF16),
            pltpu.SemaphoreType.DMA((count + 1,)),
        ],
        compiler_params=params(20),
        cost_estimate=brief(),
        name="near_codes",
    )(ids.astype(jnp.int32), tokens, variant, in_hbm(near), near_variant, in_hbm(down), *after)


def codes(sets, weights, ids, column, dtypes, after, fetch=False):
    depth, width = weights[0].shape[1:]
    sizes = [w.shape[0] for w in weights]
    has_start = [start is not None for _, _, start in sets]
    pair = max(1, 256 // width)
    chunk = 256

    def body(ids_ref, *refs):
        refs = list(refs)
        inputs = []
        for started in has_start:
            inputs.append([refs.pop(0) for _ in range(3 if started else 2)])
        flat = [w.at[j] for w, size in zip(refs[: len(sizes)], sizes) for j in range(size)]
        if fetch:
            kept_ref, sem = refs[-2:]
            copy = pltpu.make_async_copy(inputs[-1][0], kept_ref, sem)
            copy.start()
            inputs[-1][0] = kept_ref
            refs = refs[:-2]
        outs = refs[-len(sets) :]
        groups = [flat[at : at + pair] for at in range(0, len(flat), pair)]
        for n, (out_ref, given) in enumerate(zip(outs, inputs)):
            if fetch and n == len(sets) - 1:
                copy.wait()
            for row in range(0, out_ref.shape[0], chunk):
                here = slice(row, row + chunk)
                x, variant = given[0][here], given[1][here]
                if len(given) == 3:
                    kept = given[2][here, column : column + width]
                else:
                    kept = jnp.zeros((x.shape[0], width), F32)
                for g, group in enumerate(groups):
                    w = jnp.concatenate([entry[...] for entry in group], axis=1)
                    product = jnp.dot(x, w, preferred_element_type=F32)
                    for j in range(len(group)):
                        mine = variant == ids_ref[g * pair + j]
                        kept = jnp.where(mine, product[:, j * width : (j + 1) * width], kept)
                out_ref[here] = kept.astype(out_ref.dtype)

    operands, specs = [], []
    for n, (tokens, variant, start) in enumerate(sets):
        last = fetch and n == len(sets) - 1
        operands += [in_hbm(tokens) if last else tokens, variant]
        specs += [ANY if last else WHOLE, WHOLE]
        if start is not None:
            operands.append(start)
            specs.append(WHOLE)
    shapes = [
        in_vmem((tokens.shape[0], width), dtype) for (tokens, _, _), dtype in zip(sets, dtypes)
    ]
    if fetch:
        shapes.append(in_vmem(sets[-1][0].shape, BF16))
    return pl.pallas_call(
        body,
        out_shape=shapes,
        in_specs=[SCALARS] + specs + [WHOLE] * len(weights) + [ANY] * len(after),
        out_specs=[WHOLE] * len(shapes),
        scratch_shapes=[pltpu.SemaphoreType.DMA(())] if fetch else [],
        compiler_params=params(20),
        cost_estimate=brief(),
        name="codes",
    )(ids.astype(jnp.int32), *operands, *weights, *after)


def cached(queries, kv_cache, lengths, first, rows, after):
    features = queries.shape[1]
    positions, width = kv_cache.shape[1:]
    kv_local = width // (2 * HEAD)
    group = features // HEAD // kv_local
    scale = HEAD ** (-0.5)
    near = 128 // positions
    block = 64
    blocks = rows // block

    def body(len_ref, q_ref, kv_ref, *refs):
        out_ref, lse_ref, held, sems = refs[-4:]
        loads = []
        for b in range(blocks):
            lines = pl.ds(b * block, block)
            source = kv_ref.at[pl.ds(first + b * block, block)]
            loads.append(pltpu.make_async_copy(source, held.at[lines], sems.at[b]))
            loads[-1].start()
        lane = lax.broadcasted_iota(jnp.int32, (near, 128), 1)
        sublane = lax.broadcasted_iota(jnp.int32, (near, 128), 0)
        same = lane // positions == sublane
        at = lane % positions
        ones = jnp.ones((128, HEAD), BF16)

        def part(base):
            here = pl.ds(base, 2 * near)
            there = pl.ds(first + base, 2 * near)
            lines = [pl.ds(base + half * near, near) for half in range(2)]
            seen = [
                same & (at < len_ref[pl.ds((first + base) // near + half, 1), :])
                for half in range(2)
            ]
            table = [jnp.zeros((near, 128), F32) for _ in range(2)]
            for g in range(kv_local):
                at_key, at_value = 2 * g * HEAD, (2 * g + 1) * HEAD
                keys = held[here, :, at_key : at_key + HEAD].reshape(256, HEAD)
                values = held[here, :, at_value : at_value + HEAD].reshape(256, HEAD)
                heads = [slice((g * group + h) * HEAD, (g * group + h + 1) * HEAD) for h in range(group)]
                query = jnp.concatenate([q_ref[there, columns] for columns in heads], axis=0)
                scores = lax.dot_general(
                    query, keys, (((1,), (1,)), ((), ())), preferred_element_type=F32
                ).reshape(group, 2, near, 256)
                results = []
                for half in range(2):
                    own = scores[:, half, :, half * 128 : (half + 1) * 128] * scale
                    own = jnp.where(seen[half][None], own, jnp.float32(-1e30))
                    largest = jnp.max(own, axis=-1, keepdims=True)
                    weight = jnp.exp(own - largest).astype(BF16).reshape(group * near, 128)
                    value = jnp.concatenate([values[half * 128 : (half + 1) * 128], ones], axis=1)
                    mixed = jnp.dot(weight, value, preferred_element_type=F32)
                    total = mixed[:, HEAD:]
                    results.append((mixed[:, :HEAD] / total).reshape(group, near, HEAD))
                    lse = largest + jnp.log(total).reshape(group, near, 128)
                    for h in range(group):
                        table[half] = jnp.where(lane == g * group + h, lse[h], table[half])
                both = jnp.stack(results, axis=1).reshape(group, 2 * near, HEAD).astype(BF16)
                for h, columns in enumerate(heads):
                    out_ref[here, columns] = both[h]
            for half in range(2):
                lse_ref[lines[half], :] = table[half]

        def step(b, carry):
            lines = pl.ds(pl.multiple_of(b * block, block), block)
            pltpu.make_async_copy(kv_ref.at[lines], held.at[lines], sems.at[b]).wait()
            for base in range(0, block, 2 * near):
                part(pl.multiple_of(b * block + base, 2 * near))
            return carry

        lax.fori_loop(0, blocks, step, 0)

    return pl.pallas_call(
        body,
        out_shape=[in_vmem((rows, features), BF16), in_vmem((rows, 128), F32)],
        in_specs=[WHOLE, WHOLE, ANY] + [ANY] * len(after),
        out_specs=[WHOLE, WHOLE],
        scratch_shapes=[
            pltpu.VMEM((rows,) + kv_cache.shape[1:], BF16),
            pltpu.SemaphoreType.DMA((blocks,)),
        ],
        compiler_params=params(20),
        cost_estimate=brief(),
        name="cached",
    )(lengths, queries, in_hbm(kv_cache), *after)


def gather_up(terms, flags, ups, after):
    sizes = [up.shape[0] for up in ups]

    def body(flags_ref, *refs):
        term_refs, up_refs = refs[: len(terms)], refs[len(terms) : len(terms) + len(ups)]
        base_ref, up_ref, sems = refs[-3:]
        copies, at = [], 0
        for n, size in enumerate(sizes):
            copies.append(
                pltpu.make_async_copy(up_refs[n], up_ref.at[pl.ds(at, size)], sems.at[n])
            )
            copies[-1].start()
            at += size
        total = jnp.zeros(base_ref.shape, F32)
        for n, term_ref in enumerate(term_refs):
            total = total + jnp.where(flags_ref[n] == 1, term_ref[...].astype(F32), 0.0)
        base_ref[...] = total
        for copy in copies:
            copy.wait()

    return pl.pallas_call(
        body,
        out_shape=[
            in_vmem(terms[0].shape, F32),
            in_vmem((sum(sizes),) + ups[0].shape[1:], BF16),
        ],
        in_specs=[SCALARS] + [WHOLE] * len(terms) + [ANY] * (len(ups) + len(after)),
        out_specs=[WHOLE, WHOLE],
        scratch_shapes=[pltpu.SemaphoreType.DMA((len(ups),))],
        compiler_params=params(20),
        cost_estimate=brief(),
        name="gather_up",
    )(jnp.stack([jnp.int32(flag) for flag in flags]), *terms, *ups, *after)


def finish(variant_ids, queries, ranges, base, codes_a, codes_b, up, ids):
    rows, features = queries.shape
    width = base.shape[1]
    heads = features // HEAD
    group = features * 2 // width
    chunk = 128
    scale = HEAD ** (-0.5)
    counts = [len(codes_a), len(codes_b)]
    firsts = [0]
    for out1, _ in ranges:
        firsts.append(firsts[-1] + out1.shape[0])

    def body(ids_ref, variant_ref, q_ref, base_ref, up_ref, *refs):
        refs = list(refs)
        done = [(refs.pop(0), refs.pop(0)) for _ in ranges]
        a_refs, b_refs = refs[: counts[0]], refs[counts[0] : counts[0] + counts[1]]
        fresh_ref, attended_ref, fresh_made, attended_made, sems = refs[-5:]
        ones = jnp.ones((2 * HEAD, HEAD), BF16)

        def total(parts, here):
            result = parts[0][here].astype(F32)
            for part in parts[1:]:
                result = result + part[here].astype(F32)
            return result

        stores = []
        for at in range(0, rows, chunk):
            here = slice(at, at + chunk)
            which = max(n for n in range(len(ranges)) if firsts[n] <= at)
            out1_ref, lse_ref = done[which]
            inner = slice(at - firsts[which], at - firsts[which] + chunk)
            variant = variant_ref[here]
            code = jnp.concatenate(
                [total(a_refs, here).astype(BF16), total(b_refs, here).astype(BF16)], axis=1
            )
            masked = [
                jnp.where(variant == ids_ref[entry], code, jnp.zeros_like(code))
                for entry in range(up_ref.shape[0])
            ]
            change = jnp.dot(
                jnp.concatenate(masked, axis=1),
                up_ref[...].reshape(-1, width),
                preferred_element_type=F32,
            )
            fresh = (base_ref[here] + change.astype(BF16).astype(F32)).astype(BF16)
            fresh_made[here] = fresh
            keys, values = [], []
            for g in range(width // (2 * HEAD)):
                keys.append(fresh[:, 2 * g * HEAD : (2 * g + 1) * HEAD].astype(F32))
                values.append(fresh[:, (2 * g + 1) * HEAD : (2 * g + 2) * HEAD].astype(F32))
            for h in range(heads):
                columns = slice(h * HEAD, (h + 1) * HEAD)
                product = q_ref[here, columns].astype(F32) * keys[h // group]
                high = product.astype(BF16)
                low = (product - high.astype(F32)).astype(BF16)
                score = jnp.dot(
                    jnp.concatenate([high, low], axis=1), ones, preferred_element_type=F32
                )
                weight = 1.0 / (1.0 + jnp.exp(lse_ref[inner, h : h + 1] - score * scale))
                old = out1_ref[inner, columns].astype(F32)
                moved = old + weight * (values[h // group] - old)
                attended_made[here, columns] = moved.astype(BF16)
            for k, (made, ref) in enumerate(
                ((fresh_made, fresh_ref), (attended_made, attended_ref))
            ):
                lines = pl.ds(at, chunk)
                stores.append(
                    pltpu.make_async_copy(made.at[lines], ref.at[lines], sems.at[k, at // chunk])
                )
                stores[-1].start()
        for store in stores:
            store.wait()

    operands = [variant_ids, queries, base, up]
    for pieces in ranges:
        operands += pieces
    operands += [*codes_a, *codes_b]
    return pl.pallas_call(
        body,
        out_shape=[
            jax.ShapeDtypeStruct((rows, width), BF16),
            jax.ShapeDtypeStruct((rows, features), BF16),
        ],
        in_specs=[SCALARS] + [WHOLE] * len(operands),
        out_specs=[ANY, ANY],
        scratch_shapes=[
            pltpu.VMEM((rows, width), BF16),
            pltpu.VMEM((rows, features), BF16),
            pltpu.SemaphoreType.DMA((2, rows // chunk)),
        ],
        compiler_params=params(20),
        cost_estimate=brief(),
        name="finish",
    )(ids.astype(jnp.int32), *operands)


def all_reduce(value, after=()):
    size = lax.axis_size("tensor")
    bit = 1
    terms = [value]
    while bit < size:
        if len(terms) > 1:
            terms = [added(terms)]
            if after:
                terms = [gate(terms[0], after)]
        terms.append(swap(terms[0], "tensor", bit))
        bit *= 2
    return terms


def reduce_parts(parts):
    size = lax.axis_size("tensor")
    parts = {t: [part] for t, part in parts.items()}
    bit = 1
    while bit < size:
        for t in range(size - 1, 0, -1):
            if t & bit and t & (bit - 1) == 0:
                total = parts[t][0] if len(parts[t]) == 1 else added(parts[t])
                parts[t ^ bit].append(swap(total, "tensor", bit))
        bit *= 2
    return parts[0]


def general(tokens, queries, kv_cache, lengths, variant_ids, base_weight, delta_down, delta_up):
    size, me = lax.axis_size("tensor"), lax.axis_index("tensor")
    width = base_weight.shape[1] // size
    owners = lax.axis_size("adapter")
    variants, _, rank = delta_down.shape
    half = rank // 2
    every = lax.all_gather(delta_down, "adapter", axis=0, tiled=True)
    up = lax.all_gather(delta_up, "adapter", axis=0, tiled=True)
    order = sorted(range(size), key=lambda t: (-(t & 1), -t))
    parts = project(tokens, base_weight, [me ^ t for t in order], width, [])
    base_terms = reduce_parts(dict(zip(order, parts)))
    ids = jnp.arange(owners * variants, dtype=jnp.int32)
    rows_of = [(tokens, variant_ids, None)]
    codes_a, codes_b = [
        all_reduce(codes(rows_of, [every[:, :, at : at + half]], ids, 0, [BF16], parts[:1])[0])
        for at in (0, half)
    ]
    ranges = [cached(queries, kv_cache, lengths, 0, tokens.shape[0], parts[:1])]
    base, up = gather_up(base_terms, [1] * len(base_terms), [up], [])
    return finish(variant_ids, queries, ranges, base, codes_a, codes_b, up, ids)


def paired(tokens, queries, kv_cache, lengths, variant_ids, base_weight, delta_down, delta_up):
    me = lax.axis_index("tensor")
    mine = lax.axis_index("adapter")
    group = lax.axis_index("groups")
    width = base_weight.shape[1] // 4

    rows = tokens.shape[0]
    half = delta_down.shape[2] // 2
    near = swap(tokens, "adapter", 1)
    near_ids = swap(variant_ids, "adapter", 1)
    (first,) = cut(delta_down, [(group, 1, 0)], [])
    from_y = swap(first, "adapter", 2)
    part_3, second = project(
        tokens, base_weight, [me ^ 3], width, [first], delta_down, [(0, 2, 1)]
    )
    got_3 = swap(part_3, "tensor", 1)
    far = swap(second, "adapter", 2)
    part_1, part_2, own = project(
        tokens, base_weight, [me ^ 1, me ^ 2, me], width, [part_3]
    )
    got_1 = swap(part_1, "tensor", 1)
    from_y = gate(from_y, [own])
    from_x = swap(from_y, "groups", 1)
    start, start_near, near = near_codes(
        tokens,
        variant_ids,
        near,
        near_ids,
        delta_down,
        jnp.stack([2 * mine, 2 * mine + 1]),
        [own, from_y, lengths],
    )
    sum_2 = added([part_2, got_3])
    got_2 = swap(sum_2, "tensor", 2)
    lane = 2 * (mine ^ 2)
    both = [(tokens, variant_ids, start), (near, near_ids, start_near)]
    a, a_near = codes(
        both, [from_y, from_x], jnp.stack([lane + group, lane + 1 - group]), 0, [F32, BF16], [start]
    )
    b, b_near = codes(
        both, [far], jnp.stack([lane, lane + 1]), half, [F32, BF16], [a_near]
    )
    a = added([a, swap(a_near, "adapter", 1)])
    b = added([b, swap(b_near, "adapter", 1)])
    b = gate(b, [got_1, got_2])
    codes_a = all_reduce(a)
    early = cached(queries, kv_cache, lengths, 0, 128, [b])
    codes_b = all_reduce(b, [early[1]])
    late = cached(
        queries, kv_cache, lengths, 128, rows - 128, [early[1], codes_a[0], codes_b[0]]
    )
    ups = [delta_up] + [swap(delta_up, "adapter", bit) for bit in (2, 1, 3)]
    ids = jnp.stack([2 * (mine ^ bit) + j for bit in (0, 2, 1, 3) for j in (0, 1)])
    base, up = gather_up([own, got_1, got_2], [1, 1, 1], ups, [late[1], codes_b[0]])
    return finish(variant_ids, queries, [early, late], base, codes_a, codes_b, up, ids)


def local(tokens, queries, kv_cache, kv_lengths, variant_ids, base_weight, delta_down, delta_up):
    sizes = [lax.axis_size(axis) for axis in ("groups", "adapter", "tensor")]
    plan = paired if sizes == [2, 4, 4] and delta_down.shape[0] == 2 else general
    return tuple(
        plan(
            tokens,
            queries,
            kv_cache,
            jnp.repeat(kv_lengths, kv_cache.shape[1]).reshape(-1, 128),
            variant_ids,
            base_weight,
            delta_down,
            delta_up,
        )
    )


def solution(mesh):
    return jax.shard_map(
        local,
        mesh=mesh,
        in_specs=(
            P(("groups", "adapter"), "tensor"),
            P(("groups", "adapter"), "tensor"),
            P(("groups", "adapter"), None, "tensor"),
            P(("groups", "adapter")),
            P(("groups", "adapter"), None),
            P("tensor", None),
            P("adapter", "tensor", None),
            P("adapter", None, "tensor"),
        ),
        out_specs=(P(("groups", "adapter"), "tensor"), P(("groups", "adapter"), "tensor")),
        check_vma=False,
    )
```

```python
import functools

import jax
import jax.numpy as jnp
from jax import lax
from jax.experimental import pallas as pl
from jax.experimental.pallas import tpu as pltpu
from jax.sharding import PartitionSpec as P

HEAD = 128
BF16 = jnp.bfloat16
F32 = jnp.float32
ANY = pl.BlockSpec(memory_space=pl.ANY)
WHOLE = pl.BlockSpec(memory_space=pltpu.VMEM)
SCALARS = pl.BlockSpec(memory_space=pltpu.SMEM)


def params(mib):
    return pltpu.CompilerParams(vmem_limit_bytes=mib << 20)


def brief():
    return pl.CostEstimate(flops=1, bytes_accessed=1, transcendentals=0)


def gate(value, after):
    def body(*refs):
        del refs

    return pl.pallas_call(
        body,
        out_shape=jax.ShapeDtypeStruct(value.shape, value.dtype),
        in_specs=[ANY] * (1 + len(after)),
        out_specs=ANY,
        input_output_aliases={0: 0},
        compiler_params=params(16),
        cost_estimate=brief(),
        name="gate",
    )(value, *after)


def in_vmem(shape, dtype):
    return pltpu.VMEM(shape, dtype)


def in_hbm(value):
    return pltpu.with_memory_space_constraint(value, pltpu.HBM)


def cut(value, takes, after):
    depth, rank = value.shape[1:]
    half = rank // 2
    pieces = 2
    block = depth // pieces

    def body(first_ref, value_ref, *refs):
        outs, sems = refs[len(after) : -1], refs[-1]
        loads = []
        for n, (out_ref, (_, count, column)) in enumerate(zip(outs, takes)):
            for i in range(count):
                for k in range(pieces):
                    lines = pl.ds(k * block, block)
                    loads.append(
                        pltpu.make_async_copy(
                            value_ref.at[first_ref[n] + i, lines, pl.ds(column * half, half)],
                            out_ref.at[i, lines],
                            sems.at[n, i, k],
                        )
                    )
        for load in loads:
            load.start()
        for load in loads:
            load.wait()

    return pl.pallas_call(
        body,
        out_shape=[in_vmem((count, depth, half), value.dtype) for _, count, _ in takes],
        in_specs=[SCALARS] + [ANY] * (1 + len(after)),
        out_specs=[WHOLE] * len(takes),
        scratch_shapes=[
            pltpu.SemaphoreType.DMA((len(takes), max(count for _, count, _ in takes), pieces))
        ],
        compiler_params=params(16),
        cost_estimate=brief(),
        name="cut",
    )(jnp.stack([jnp.int32(first) for first, _, _ in takes]), in_hbm(value), *after)


def swap(value, axis, bit):
    return lax.ppermute(value, axis, [(i, i ^ bit) for i in range(lax.axis_size(axis))])


def added(terms):
    return sum(term.astype(F32) for term in terms).astype(BF16)


def project(tokens, weight, shards, width, after, down=None, takes=(), near_adds=()):
    rows, depth = tokens.shape
    count = len(shards)
    pieces = 4
    block = depth // pieces
    extra = 1 if takes else 0

    def body(scalars_ref, x_ref, w_ref, *refs):
        down_ref = refs[0] if extra else None
        refs = refs[extra + len(after) :]
        outs, cuts = refs[:count], refs[count : count + len(takes)]
        refs = refs[count + len(takes) :]
        token_ref, held, made, load_sems, store_sems = refs[:5]
        scratch = refs[5:]
        token_ref[...] = jnp.zeros_like(token_ref)
        loads = [
            [
                pltpu.make_async_copy(
                    w_ref.at[
                        pl.ds(k * block, block),
                        pl.ds(pl.multiple_of(scalars_ref[i] * width, width), width),
                    ],
                    held.at[i, pl.ds(k * block, block)],
                    load_sems.at[i, k],
                )
                for k in range(pieces)
            ]
            for i in range(count)
        ]
        stores = [
            pltpu.make_async_copy(made.at[i], outs[i], store_sems.at[i])
            for i in range(count)
            if i not in near_adds
        ]
        cut_in, cut_out = [], []
        for n, (_, size, column) in enumerate(takes):
            spot, sems = scratch[n], scratch[len(takes)]
            half = spot.shape[2]
            start = scalars_ref[count + n]
            cut_in.append(
                pltpu.make_async_copy(
                    down_ref.at[pl.ds(start, size), :, pl.ds(column * half, half)],
                    spot,
                    sems.at[n, 0],
                )
            )
            cut_out.append(pltpu.make_async_copy(spot, cuts[n], sems.at[n, 1]))
        for copy in cut_in[:1]:
            copy.start()
        for group in loads:
            for load in group:
                load.start()
        for copy in cut_in[1:]:
            copy.start()
        for i in range(count):
            if i == 0:
                total = jnp.zeros((rows, width), F32)
                for k in range(pieces):
                    loads[0][k].wait()
                    part = slice(k * block, (k + 1) * block)
                    total = total + jnp.dot(
                        x_ref[:, part], held[0, part], preferred_element_type=F32
                    )
                result = total.astype(BF16)
            else:
                for k in range(pieces):
                    loads[i][k].wait()
                result = jnp.dot(x_ref[...], held[i], preferred_element_type=F32).astype(BF16)
            if i in near_adds:
                outs[i][...] = result
            else:
                made[i] = result
                stores[sum(1 for n in range(i) if n not in near_adds)].start()
            if i == 0:
                for copy, out in zip(cut_in, cut_out):
                    copy.wait()
                    out.start()
        for store in stores + cut_out:
            store.wait()

    shapes = [
        (in_vmem if i in near_adds else pltpu.HBM)((rows, width), BF16) for i in range(count)
    ]
    scratch = [
        pltpu.VMEM((count, depth, width), BF16),
        pltpu.VMEM((count, rows, width), BF16),
        pltpu.SemaphoreType.DMA((count, pieces)),
        pltpu.SemaphoreType.DMA((count,)),
    ]
    operands = [tokens, in_hbm(weight)]
    scalars = list(shards)
    if extra:
        operands.append(in_hbm(down))
        for first, size, _ in takes:
            piece = (size, depth, down.shape[2] // 2)
            shapes.append(pltpu.HBM(piece, BF16))
            scratch.append(pltpu.VMEM(piece, BF16))
            scalars.append(first)
        scratch.append(pltpu.SemaphoreType.DMA((len(takes), 2)))
    shapes.append(jax.ShapeDtypeStruct((8, 128), F32))
    return pl.pallas_call(
        body,
        out_shape=shapes,
        in_specs=[SCALARS, WHOLE] + [ANY] * (1 + extra + len(after)),
        out_specs=[WHOLE if i in near_adds else ANY for i in range(len(shapes) - 1)] + [WHOLE],
        scratch_shapes=scratch,
        compiler_params=params(20),
        cost_estimate=brief(),
        name="project",
    )(jnp.stack([jnp.int32(n) for n in scalars]), *operands, *after)


def near_codes(tokens, variant, near, near_variant, down, ids, after):
    rows, depth = tokens.shape
    count, _, rank = down.shape
    chunk = 256

    def body(ids_ref, x_ref, variant_ref, near_ref, near_variant_ref, down_ref, *refs):
        out_ref, near_out_ref, kept_ref, held, sems = refs[-5:]
        loads = [
            pltpu.make_async_copy(down_ref.at[j], held.at[j], sems.at[j]) for j in range(count)
        ]
        copy = pltpu.make_async_copy(near_ref, kept_ref, sems.at[count])
        loads[0].start()
        copy.start()
        for load in loads[1:]:
            load.start()
        for j in range(count):
            loads[j].wait()
            for source, named, result in (
                (x_ref, variant_ref, out_ref),
                (kept_ref, near_variant_ref, near_out_ref),
            ):
                if j == 0 and source is kept_ref:
                    copy.wait()
                for row in range(0, rows, chunk):
                    here = slice(row, row + chunk)
                    product = jnp.dot(source[here], held[j], preferred_element_type=F32)
                    other = result[here] if j > 0 else jnp.zeros_like(product)
                    result[here] = jnp.where(named[here] == ids_ref[j], product, other)

    return pl.pallas_call(
        body,
        out_shape=[
            in_vmem((rows, rank), F32),
            in_vmem((rows, rank), F32),
            in_vmem((rows, depth), BF16),
        ],
        in_specs=[SCALARS, WHOLE, WHOLE, ANY, WHOLE, ANY] + [ANY] * len(after),
        out_specs=[WHOLE] * 3,
        scratch_shapes=[
            pltpu.VMEM(down.shape, BF16),
            pltpu.SemaphoreType.DMA((count + 1,)),
        ],
        compiler_params=params(20),
        cost_estimate=brief(),
        name="near_codes",
    )(ids.astype(jnp.int32), tokens, variant, in_hbm(near), near_variant, in_hbm(down), *after)


def codes(sets, weights, ids, column, dtypes, after, fetch=False):
    depth, width = weights[0].shape[1:]
    sizes = [w.shape[0] for w in weights]
    has_start = [start is not None for _, _, start in sets]
    pair = max(1, 256 // width)
    chunk = 256

    def body(ids_ref, *refs):
        refs = list(refs)
        inputs = []
        for started in has_start:
            inputs.append([refs.pop(0) for _ in range(3 if started else 2)])
        flat = [w.at[j] for w, size in zip(refs[: len(sizes)], sizes) for j in range(size)]
        if fetch:
            kept_ref, sem = refs[-2:]
            copy = pltpu.make_async_copy(inputs[-1][0], kept_ref, sem)
            copy.start()
            inputs[-1][0] = kept_ref
            refs = refs[:-2]
        outs = refs[-len(sets) :]
        groups = [flat[at : at + pair] for at in range(0, len(flat), pair)]
        for n, (out_ref, given) in enumerate(zip(outs, inputs)):
            if fetch and n == len(sets) - 1:
                copy.wait()
            for row in range(0, out_ref.shape[0], chunk):
                here = slice(row, row + chunk)
                x, variant = given[0][here], given[1][here]
                if len(given) == 3:
                    kept = given[2][here, column : column + width]
                else:
                    kept = jnp.zeros((x.shape[0], width), F32)
                for g, group in enumerate(groups):
                    w = jnp.concatenate([entry[...] for entry in group], axis=1)
                    product = jnp.dot(x, w, preferred_element_type=F32)
                    for j in range(len(group)):
                        mine = variant == ids_ref[g * pair + j]
                        kept = jnp.where(mine, product[:, j * width : (j + 1) * width], kept)
                out_ref[here] = kept.astype(out_ref.dtype)

    operands, specs = [], []
    for n, (tokens, variant, start) in enumerate(sets):
        last = fetch and n == len(sets) - 1
        operands += [in_hbm(tokens) if last else tokens, variant]
        specs += [ANY if last else WHOLE, WHOLE]
        if start is not None:
            operands.append(start)
            specs.append(WHOLE)
    shapes = [
        in_vmem((tokens.shape[0], width), dtype) for (tokens, _, _), dtype in zip(sets, dtypes)
    ]
    if fetch:
        shapes.append(in_vmem(sets[-1][0].shape, BF16))
    return pl.pallas_call(
        body,
        out_shape=shapes,
        in_specs=[SCALARS] + specs + [WHOLE] * len(weights) + [ANY] * len(after),
        out_specs=[WHOLE] * len(shapes),
        scratch_shapes=[pltpu.SemaphoreType.DMA(())] if fetch else [],
        compiler_params=params(20),
        cost_estimate=brief(),
        name="codes",
    )(ids.astype(jnp.int32), *operands, *weights, *after)


def cached(queries, kv_cache, lengths, first, rows, after):
    features = queries.shape[1]
    positions, width = kv_cache.shape[1:]
    kv_local = width // (2 * HEAD)
    group = features // HEAD // kv_local
    scale = HEAD ** (-0.5)
    near = 128 // positions
    block = 64
    blocks = rows // block

    def body(len_ref, q_ref, kv_ref, *refs):
        out_ref, lse_ref, held, sems = refs[-4:]
        loads = []
        for b in range(blocks):
            lines = pl.ds(b * block, block)
            source = kv_ref.at[pl.ds(first + b * block, block)]
            loads.append(pltpu.make_async_copy(source, held.at[lines], sems.at[b]))
            loads[-1].start()
        lane = lax.broadcasted_iota(jnp.int32, (near, 128), 1)
        sublane = lax.broadcasted_iota(jnp.int32, (near, 128), 0)
        same = lane // positions == sublane
        at = lane % positions
        ones = jnp.ones((128, HEAD), BF16)

        def part(base):
            here = pl.ds(base, 2 * near)
            there = pl.ds(first + base, 2 * near)
            lines = [pl.ds(base + half * near, near) for half in range(2)]
            seen = [
                same & (at < len_ref[pl.ds((first + base) // near + half, 1), :])
                for half in range(2)
            ]
            table = [jnp.zeros((near, 128), F32) for _ in range(2)]
            for g in range(kv_local):
                at_key, at_value = 2 * g * HEAD, (2 * g + 1) * HEAD
                keys = held[here, :, at_key : at_key + HEAD].reshape(256, HEAD)
                values = held[here, :, at_value : at_value + HEAD].reshape(256, HEAD)
                heads = [slice((g * group + h) * HEAD, (g * group + h + 1) * HEAD) for h in range(group)]
                query = jnp.concatenate([q_ref[there, columns] for columns in heads], axis=0)
                scores = lax.dot_general(
                    query, keys, (((1,), (1,)), ((), ())), preferred_element_type=F32
                ).reshape(group, 2, near, 256)
                results = []
                for half in range(2):
                    own = scores[:, half, :, half * 128 : (half + 1) * 128] * scale
                    own = jnp.where(seen[half][None], own, jnp.float32(-1e30))
                    largest = jnp.max(own, axis=-1, keepdims=True)
                    weight = jnp.exp(own - largest).astype(BF16).reshape(group * near, 128)
                    value = jnp.concatenate([values[half * 128 : (half + 1) * 128], ones], axis=1)
                    mixed = jnp.dot(weight, value, preferred_element_type=F32)
                    total = mixed[:, HEAD:]
                    results.append((mixed[:, :HEAD] / total).reshape(group, near, HEAD))
                    lse = largest + jnp.log(total).reshape(group, near, 128)
                    for h in range(group):
                        table[half] = jnp.where(lane == g * group + h, lse[h], table[half])
                both = jnp.stack(results, axis=1).reshape(group, 2 * near, HEAD).astype(BF16)
                for h, columns in enumerate(heads):
                    out_ref[here, columns] = both[h]
            for half in range(2):
                lse_ref[lines[half], :] = table[half]

        def step(b, carry):
            lines = pl.ds(pl.multiple_of(b * block, block), block)
            pltpu.make_async_copy(kv_ref.at[lines], held.at[lines], sems.at[b]).wait()
            for base in range(0, block, 2 * near):
                part(pl.multiple_of(b * block + base, 2 * near))
            return carry

        lax.fori_loop(0, blocks, step, 0)

    return pl.pallas_call(
        body,
        out_shape=[in_vmem((rows, features), BF16), in_vmem((rows, 128), F32)],
        in_specs=[WHOLE, WHOLE, ANY] + [ANY] * len(after),
        out_specs=[WHOLE, WHOLE],
        scratch_shapes=[
            pltpu.VMEM((rows,) + kv_cache.shape[1:], BF16),
            pltpu.SemaphoreType.DMA((blocks,)),
        ],
        compiler_params=params(20),
        cost_estimate=brief(),
        name="cached",
    )(lengths, queries, in_hbm(kv_cache), *after)


def gather_up(terms, flags, ups, after):
    sizes = [up.shape[0] for up in ups]

    def body(flags_ref, *refs):
        term_refs, up_refs = refs[: len(terms)], refs[len(terms) : len(terms) + len(ups)]
        base_ref, up_ref, sems = refs[-3:]
        copies, at = [], 0
        for n, size in enumerate(sizes):
            copies.append(
                pltpu.make_async_copy(up_refs[n], up_ref.at[pl.ds(at, size)], sems.at[n])
            )
            copies[-1].start()
            at += size
        total = jnp.zeros(base_ref.shape, F32)
        for n, term_ref in enumerate(term_refs):
            total = total + jnp.where(flags_ref[n] == 1, term_ref[...].astype(F32), 0.0)
        base_ref[...] = total
        for copy in copies:
            copy.wait()

    return pl.pallas_call(
        body,
        out_shape=[
            in_vmem(terms[0].shape, F32),
            in_vmem((sum(sizes),) + ups[0].shape[1:], BF16),
        ],
        in_specs=[SCALARS] + [WHOLE] * len(terms) + [ANY] * (len(ups) + len(after)),
        out_specs=[WHOLE, WHOLE],
        scratch_shapes=[pltpu.SemaphoreType.DMA((len(ups),))],
        compiler_params=params(20),
        cost_estimate=brief(),
        name="gather_up",
    )(jnp.stack([jnp.int32(flag) for flag in flags]), *terms, *ups, *after)


def finish(variant_ids, queries, ranges, base, codes_a, codes_b, up, ids):
    rows, features = queries.shape
    width = base.shape[1]
    heads = features // HEAD
    group = features * 2 // width
    chunk = 128
    scale = HEAD ** (-0.5)
    counts = [len(codes_a), len(codes_b)]
    firsts = [0]
    for out1, _ in ranges:
        firsts.append(firsts[-1] + out1.shape[0])

    def body(ids_ref, variant_ref, q_ref, base_ref, up_ref, *refs):
        refs = list(refs)
        done = [(refs.pop(0), refs.pop(0)) for _ in ranges]
        a_refs, b_refs = refs[: counts[0]], refs[counts[0] : counts[0] + counts[1]]
        fresh_ref, attended_ref, fresh_made, attended_made, sems = refs[-5:]
        ones = jnp.ones((2 * HEAD, HEAD), BF16)

        def total(parts, here):
            result = parts[0][here].astype(F32)
            for part in parts[1:]:
                result = result + part[here].astype(F32)
            return result

        stores = []
        for at in range(0, rows, 2 * chunk):
            here = slice(at, at + 2 * chunk)
            variant = variant_ref[here]
            code = jnp.concatenate(
                [total(a_refs, here).astype(BF16), total(b_refs, here).astype(BF16)], axis=1
            )
            masked = [
                jnp.where(variant == ids_ref[entry], code, jnp.zeros_like(code))
                for entry in range(up_ref.shape[0])
            ]
            change = jnp.dot(
                jnp.concatenate(masked, axis=1),
                up_ref[...].reshape(-1, width),
                preferred_element_type=F32,
            )
            fresh = (base_ref[here] + change.astype(BF16).astype(F32)).astype(BF16)
            fresh_made[here] = fresh
        for at in range(0, rows, chunk):
            here = slice(at, at + chunk)
            which = max(n for n in range(len(ranges)) if firsts[n] <= at)
            out1_ref, lse_ref = done[which]
            inner = slice(at - firsts[which], at - firsts[which] + chunk)
            fresh = fresh_made[here]
            keys, values = [], []
            for g in range(width // (2 * HEAD)):
                keys.append(fresh[:, 2 * g * HEAD : (2 * g + 1) * HEAD].astype(F32))
                values.append(fresh[:, (2 * g + 1) * HEAD : (2 * g + 2) * HEAD].astype(F32))
            for h in range(heads):
                columns = slice(h * HEAD, (h + 1) * HEAD)
                product = q_ref[here, columns].astype(F32) * keys[h // group]
                high = product.astype(BF16)
                low = (product - high.astype(F32)).astype(BF16)
                score = jnp.dot(
                    jnp.concatenate([high, low], axis=1), ones, preferred_element_type=F32
                )
                weight = 1.0 / (1.0 + jnp.exp(lse_ref[inner, h : h + 1] - score * scale))
                old = out1_ref[inner, columns].astype(F32)
                moved = old + weight * (values[h // group] - old)
                attended_made[here, columns] = moved.astype(BF16)
            for k, (made, ref) in enumerate(
                ((fresh_made, fresh_ref), (attended_made, attended_ref))
            ):
                lines = pl.ds(at, chunk)
                stores.append(
                    pltpu.make_async_copy(made.at[lines], ref.at[lines], sems.at[k, at // chunk])
                )
                stores[-1].start()
        for store in stores:
            store.wait()

    operands = [variant_ids, queries, base, up]
    for pieces in ranges:
        operands += pieces
    operands += [*codes_a, *codes_b]
    return pl.pallas_call(
        body,
        out_shape=[
            jax.ShapeDtypeStruct((rows, width), BF16),
            jax.ShapeDtypeStruct((rows, features), BF16),
        ],
        in_specs=[SCALARS] + [WHOLE] * len(operands),
        out_specs=[ANY, ANY],
        scratch_shapes=[
            pltpu.VMEM((rows, width), BF16),
            pltpu.VMEM((rows, features), BF16),
            pltpu.SemaphoreType.DMA((2, rows // chunk)),
        ],
        compiler_params=params(20),
        cost_estimate=brief(),
        name="finish",
    )(ids.astype(jnp.int32), *operands)


def all_reduce(value, after=()):
    size = lax.axis_size("tensor")
    bit = 1
    terms = [value]
    while bit < size:
        if len(terms) > 1:
            terms = [added(terms)]
            if after:
                terms = [gate(terms[0], after)]
        terms.append(swap(terms[0], "tensor", bit))
        bit *= 2
    return terms


def reduce_parts(parts):
    size = lax.axis_size("tensor")
    parts = {t: [part] for t, part in parts.items()}
    bit = 1
    while bit < size:
        for t in range(size - 1, 0, -1):
            if t & bit and t & (bit - 1) == 0:
                total = parts[t][0] if len(parts[t]) == 1 else added(parts[t])
                parts[t ^ bit].append(swap(total, "tensor", bit))
        bit *= 2
    return parts[0]


def general(tokens, queries, kv_cache, lengths, variant_ids, base_weight, delta_down, delta_up):
    size, me = lax.axis_size("tensor"), lax.axis_index("tensor")
    width = base_weight.shape[1] // size
    owners = lax.axis_size("adapter")
    variants, _, rank = delta_down.shape
    half = rank // 2
    every = lax.all_gather(delta_down, "adapter", axis=0, tiled=True)
    up = lax.all_gather(delta_up, "adapter", axis=0, tiled=True)
    order = sorted(range(size), key=lambda t: (-(t & 1), -t))
    *parts, token = project(tokens, base_weight, [me ^ t for t in order], width, [])
    base_terms = reduce_parts(dict(zip(order, parts)))
    ids = jnp.arange(owners * variants, dtype=jnp.int32)
    rows_of = [(tokens, variant_ids, None)]
    codes_a, codes_b = [
        all_reduce(codes(rows_of, [every[:, :, at : at + half]], ids, 0, [BF16], [token])[0])
        for at in (0, half)
    ]
    ranges = [cached(queries, kv_cache, lengths, 0, tokens.shape[0], [token])]
    base, up = gather_up(base_terms, [1] * len(base_terms), [up], [])
    return finish(variant_ids, queries, ranges, base, codes_a, codes_b, up, ids)


def paired(tokens, queries, kv_cache, lengths, variant_ids, base_weight, delta_down, delta_up):
    me = lax.axis_index("tensor")
    mine = lax.axis_index("adapter")
    group = lax.axis_index("groups")
    width = base_weight.shape[1] // 4

    rows = tokens.shape[0]
    half = delta_down.shape[2] // 2
    near = swap(tokens, "adapter", 1)
    near_ids = swap(variant_ids, "adapter", 1)
    (first,) = cut(delta_down, [(group, 1, 0)], [])
    from_y = swap(first, "adapter", 2)
    part_3, second, token = project(
        tokens, base_weight, [me ^ 3], width, [first], delta_down, [(0, 2, 1)]
    )
    got_3 = swap(part_3, "tensor", 1)
    far = swap(second, "adapter", 2)
    part_1, part_2, own, token = project(
        tokens, base_weight, [me ^ 1, me ^ 2, me], width, [token]
    )
    got_1 = swap(part_1, "tensor", 1)
    from_y = gate(from_y, [token])
    from_x = swap(from_y, "groups", 1)
    start, start_near, near = near_codes(
        tokens,
        variant_ids,
        near,
        near_ids,
        delta_down,
        jnp.stack([2 * mine, 2 * mine + 1]),
        [token, from_y, lengths],
    )
    sum_2 = added([part_2, got_3])
    got_2 = swap(sum_2, "tensor", 2)
    lane = 2 * (mine ^ 2)
    both = [(tokens, variant_ids, start), (near, near_ids, start_near)]
    a, a_near = codes(
        both, [from_y, from_x], jnp.stack([lane + group, lane + 1 - group]), 0, [F32, BF16], [start]
    )
    b, b_near = codes(
        both, [far], jnp.stack([lane, lane + 1]), half, [F32, BF16], [a_near]
    )
    a = added([a, swap(a_near, "adapter", 1)])
    b = added([b, swap(b_near, "adapter", 1)])
    b = gate(b, [got_1, got_2])
    codes_a = all_reduce(a)
    early = cached(queries, kv_cache, lengths, 0, 128, [b])
    codes_b = all_reduce(b, [early[1]])
    late = cached(
        queries, kv_cache, lengths, 128, rows - 128, [early[1], codes_a[0], codes_b[0]]
    )
    ups = [delta_up] + [swap(delta_up, "adapter", bit) for bit in (2, 1, 3)]
    ids = jnp.stack([2 * (mine ^ bit) + j for bit in (0, 2, 1, 3) for j in (0, 1)])
    base, up = gather_up([own, got_1, got_2], [1, 1, 1], ups, [late[1], codes_b[0]])
    return finish(variant_ids, queries, [early, late], base, codes_a, codes_b, up, ids)


def local(tokens, queries, kv_cache, kv_lengths, variant_ids, base_weight, delta_down, delta_up):
    sizes = [lax.axis_size(axis) for axis in ("groups", "adapter", "tensor")]
    plan = paired if sizes == [2, 4, 4] and delta_down.shape[0] == 2 else general
    return tuple(
        plan(
            tokens,
            queries,
            kv_cache,
            jnp.repeat(kv_lengths, kv_cache.shape[1]).reshape(-1, 128),
            variant_ids,
            base_weight,
            delta_down,
            delta_up,
        )
    )


def solution(mesh):
    return jax.shard_map(
        local,
        mesh=mesh,
        in_specs=(
            P(("groups", "adapter"), "tensor"),
            P(("groups", "adapter"), "tensor"),
            P(("groups", "adapter"), None, "tensor"),
            P(("groups", "adapter")),
            P(("groups", "adapter"), None),
            P("tensor", None),
            P("adapter", "tensor", None),
            P("adapter", None, "tensor"),
        ),
        out_specs=(P(("groups", "adapter"), "tensor"), P(("groups", "adapter"), "tensor")),
        check_vma=False,
    )
```

```python
import functools

import jax
import jax.numpy as jnp
from jax import lax
from jax.experimental import pallas as pl
from jax.experimental.pallas import tpu as pltpu
from jax.sharding import PartitionSpec as P

HEAD = 128
BF16 = jnp.bfloat16
F32 = jnp.float32
ANY = pl.BlockSpec(memory_space=pl.ANY)
WHOLE = pl.BlockSpec(memory_space=pltpu.VMEM)
SCALARS = pl.BlockSpec(memory_space=pltpu.SMEM)


def params(mib):
    return pltpu.CompilerParams(vmem_limit_bytes=mib << 20)


def brief():
    return pl.CostEstimate(flops=1, bytes_accessed=1, transcendentals=0)


def gate(value, after):
    def body(*refs):
        del refs

    return pl.pallas_call(
        body,
        out_shape=jax.ShapeDtypeStruct(value.shape, value.dtype),
        in_specs=[ANY] * (1 + len(after)),
        out_specs=ANY,
        input_output_aliases={0: 0},
        compiler_params=params(16),
        cost_estimate=brief(),
        name="gate",
    )(value, *after)


def in_vmem(shape, dtype):
    return pltpu.VMEM(shape, dtype)


def in_hbm(value):
    return pltpu.with_memory_space_constraint(value, pltpu.HBM)


def cut(value, takes, after):
    depth, rank = value.shape[1:]
    half = rank // 2
    pieces = 2
    block = depth // pieces

    def body(first_ref, value_ref, *refs):
        outs, sems = refs[len(after) : -1], refs[-1]
        loads = []
        for n, (out_ref, (_, count, column)) in enumerate(zip(outs, takes)):
            for i in range(count):
                for k in range(pieces):
                    lines = pl.ds(k * block, block)
                    loads.append(
                        pltpu.make_async_copy(
                            value_ref.at[first_ref[n] + i, lines, pl.ds(column * half, half)],
                            out_ref.at[i, lines],
                            sems.at[n, i, k],
                        )
                    )
        for load in loads:
            load.start()
        for load in loads:
            load.wait()

    return pl.pallas_call(
        body,
        out_shape=[in_vmem((count, depth, half), value.dtype) for _, count, _ in takes],
        in_specs=[SCALARS] + [ANY] * (1 + len(after)),
        out_specs=[WHOLE] * len(takes),
        scratch_shapes=[
            pltpu.SemaphoreType.DMA((len(takes), max(count for _, count, _ in takes), pieces))
        ],
        compiler_params=params(16),
        cost_estimate=brief(),
        name="cut",
    )(jnp.stack([jnp.int32(first) for first, _, _ in takes]), in_hbm(value), *after)


def swap(value, axis, bit):
    return lax.ppermute(value, axis, [(i, i ^ bit) for i in range(lax.axis_size(axis))])


def added(terms):
    return sum(term.astype(F32) for term in terms).astype(BF16)


def project(tokens, weight, shards, width, after, down=None, takes=(), near_adds=()):
    rows, depth = tokens.shape
    count = len(shards)
    pieces = 4
    block = depth // pieces
    extra = 1 if takes else 0

    def body(scalars_ref, x_ref, w_ref, *refs):
        down_ref = refs[0] if extra else None
        refs = refs[extra + len(after) :]
        outs, cuts = refs[:count], refs[count : count + len(takes)]
        refs = refs[count + len(takes) :]
        token_ref, held, made, load_sems, store_sems = refs[:5]
        scratch = refs[5:]
        token_ref[...] = jnp.zeros_like(token_ref)
        loads = [
            [
                pltpu.make_async_copy(
                    w_ref.at[
                        pl.ds(k * block, block),
                        pl.ds(pl.multiple_of(scalars_ref[i] * width, width), width),
                    ],
                    held.at[i, pl.ds(k * block, block)],
                    load_sems.at[i, k],
                )
                for k in range(pieces)
            ]
            for i in range(count)
        ]
        stores = [
            pltpu.make_async_copy(made.at[i], outs[i], store_sems.at[i])
            for i in range(count)
            if i not in near_adds
        ]
        cut_in, cut_out = [], []
        for n, (_, size, column) in enumerate(takes):
            spot, sems = scratch[n], scratch[len(takes)]
            half = spot.shape[2]
            start = scalars_ref[count + n]
            cut_in.append(
                pltpu.make_async_copy(
                    down_ref.at[pl.ds(start, size), :, pl.ds(column * half, half)],
                    spot,
                    sems.at[n, 0],
                )
            )
            cut_out.append(pltpu.make_async_copy(spot, cuts[n], sems.at[n, 1]))
        for copy in cut_in[:1]:
            copy.start()
        for group in loads:
            for load in group:
                load.start()
        for copy in cut_in[1:]:
            copy.start()
        for i in range(count):
            if i == 0:
                total = jnp.zeros((rows, width), F32)
                for k in range(pieces):
                    loads[0][k].wait()
                    part = slice(k * block, (k + 1) * block)
                    total = total + jnp.dot(
                        x_ref[:, part], held[0, part], preferred_element_type=F32
                    )
                result = total.astype(BF16)
            else:
                for k in range(pieces):
                    loads[i][k].wait()
                result = jnp.dot(x_ref[...], held[i], preferred_element_type=F32).astype(BF16)
            if i in near_adds:
                outs[i][...] = result
            else:
                made[i] = result
                stores[sum(1 for n in range(i) if n not in near_adds)].start()
            if i == 0:
                for copy, out in zip(cut_in, cut_out):
                    copy.wait()
                    out.start()
        for store in stores + cut_out:
            store.wait()

    shapes = [
        (in_vmem if i in near_adds else pltpu.HBM)((rows, width), BF16) for i in range(count)
    ]
    scratch = [
        pltpu.VMEM((count, depth, width), BF16),
        pltpu.VMEM((count, rows, width), BF16),
        pltpu.SemaphoreType.DMA((count, pieces)),
        pltpu.SemaphoreType.DMA((count,)),
    ]
    operands = [tokens, in_hbm(weight)]
    scalars = list(shards)
    if extra:
        operands.append(in_hbm(down))
        for first, size, _ in takes:
            piece = (size, depth, down.shape[2] // 2)
            shapes.append(pltpu.HBM(piece, BF16))
            scratch.append(pltpu.VMEM(piece, BF16))
            scalars.append(first)
        scratch.append(pltpu.SemaphoreType.DMA((len(takes), 2)))
    shapes.append(jax.ShapeDtypeStruct((8, 128), F32))
    return pl.pallas_call(
        body,
        out_shape=shapes,
        in_specs=[SCALARS, WHOLE] + [ANY] * (1 + extra + len(after)),
        out_specs=[WHOLE if i in near_adds else ANY for i in range(len(shapes) - 1)] + [WHOLE],
        scratch_shapes=scratch,
        compiler_params=params(20),
        cost_estimate=brief(),
        name="project",
    )(jnp.stack([jnp.int32(n) for n in scalars]), *operands, *after)


def near_codes(tokens, variant, near, near_variant, down, ids, after):
    rows, depth = tokens.shape
    count, _, rank = down.shape
    chunk = 256

    def body(ids_ref, x_ref, variant_ref, near_ref, near_variant_ref, down_ref, *refs):
        out_ref, near_out_ref, kept_ref, held, sems = refs[-5:]
        loads = [
            pltpu.make_async_copy(down_ref.at[j], held.at[j], sems.at[j]) for j in range(count)
        ]
        copy = pltpu.make_async_copy(near_ref, kept_ref, sems.at[count])
        loads[0].start()
        copy.start()
        for load in loads[1:]:
            load.start()
        for j in range(count):
            loads[j].wait()
            for source, named, result in (
                (x_ref, variant_ref, out_ref),
                (kept_ref, near_variant_ref, near_out_ref),
            ):
                if j == 0 and source is kept_ref:
                    copy.wait()
                for row in range(0, rows, chunk):
                    here = slice(row, row + chunk)
                    product = jnp.dot(source[here], held[j], preferred_element_type=F32)
                    other = result[here] if j > 0 else jnp.zeros_like(product)
                    result[here] = jnp.where(named[here] == ids_ref[j], product, other)

    return pl.pallas_call(
        body,
        out_shape=[
            in_vmem((rows, rank), F32),
            in_vmem((rows, rank), F32),
            in_vmem((rows, depth), BF16),
        ],
        in_specs=[SCALARS, WHOLE, WHOLE, ANY, WHOLE, ANY] + [ANY] * len(after),
        out_specs=[WHOLE] * 3,
        scratch_shapes=[
            pltpu.VMEM(down.shape, BF16),
            pltpu.SemaphoreType.DMA((count + 1,)),
        ],
        compiler_params=params(20),
        cost_estimate=brief(),
        name="near_codes",
    )(ids.astype(jnp.int32), tokens, variant, in_hbm(near), near_variant, in_hbm(down), *after)


def codes(sets, weights, ids, column, dtypes, after, fetch=False):
    depth, width = weights[0].shape[1:]
    sizes = [w.shape[0] for w in weights]
    has_start = [start is not None for _, _, start in sets]
    pair = max(1, 256 // width)
    chunk = 256

    def body(ids_ref, *refs):
        refs = list(refs)
        inputs = []
        for started in has_start:
            inputs.append([refs.pop(0) for _ in range(3 if started else 2)])
        flat = [w.at[j] for w, size in zip(refs[: len(sizes)], sizes) for j in range(size)]
        if fetch:
            kept_ref, sem = refs[-2:]
            copy = pltpu.make_async_copy(inputs[-1][0], kept_ref, sem)
            copy.start()
            inputs[-1][0] = kept_ref
            refs = refs[:-2]
        outs = refs[-len(sets) :]
        groups = [flat[at : at + pair] for at in range(0, len(flat), pair)]
        for n, (out_ref, given) in enumerate(zip(outs, inputs)):
            if fetch and n == len(sets) - 1:
                copy.wait()
            for row in range(0, out_ref.shape[0], chunk):
                here = slice(row, row + chunk)
                x, variant = given[0][here], given[1][here]
                if len(given) == 3:
                    kept = given[2][here, column : column + width]
                else:
                    kept = jnp.zeros((x.shape[0], width), F32)
                for g, group in enumerate(groups):
                    w = jnp.concatenate([entry[...] for entry in group], axis=1)
                    product = jnp.dot(x, w, preferred_element_type=F32)
                    for j in range(len(group)):
                        mine = variant == ids_ref[g * pair + j]
                        kept = jnp.where(mine, product[:, j * width : (j + 1) * width], kept)
                out_ref[here] = kept.astype(out_ref.dtype)

    operands, specs = [], []
    for n, (tokens, variant, start) in enumerate(sets):
        last = fetch and n == len(sets) - 1
        operands += [in_hbm(tokens) if last else tokens, variant]
        specs += [ANY if last else WHOLE, WHOLE]
        if start is not None:
            operands.append(start)
            specs.append(WHOLE)
    shapes = [
        in_vmem((tokens.shape[0], width), dtype) for (tokens, _, _), dtype in zip(sets, dtypes)
    ]
    if fetch:
        shapes.append(in_vmem(sets[-1][0].shape, BF16))
    return pl.pallas_call(
        body,
        out_shape=shapes,
        in_specs=[SCALARS] + specs + [WHOLE] * len(weights) + [ANY] * len(after),
        out_specs=[WHOLE] * len(shapes),
        scratch_shapes=[pltpu.SemaphoreType.DMA(())] if fetch else [],
        compiler_params=params(20),
        cost_estimate=brief(),
        name="codes",
    )(ids.astype(jnp.int32), *operands, *weights, *after)


def cached(queries, kv_cache, lengths, first, rows, after):
    features = queries.shape[1]
    positions, width = kv_cache.shape[1:]
    kv_local = width // (2 * HEAD)
    group = features // HEAD // kv_local
    scale = HEAD ** (-0.5)
    near = 128 // positions
    block = 64
    blocks = rows // block

    def body(len_ref, q_ref, kv_ref, *refs):
        out_ref, lse_ref, held, sems = refs[-4:]
        loads = []
        for b in range(blocks):
            lines = pl.ds(b * block, block)
            source = kv_ref.at[pl.ds(first + b * block, block)]
            loads.append(pltpu.make_async_copy(source, held.at[lines], sems.at[b]))
            loads[-1].start()
        lane = lax.broadcasted_iota(jnp.int32, (near, 128), 1)
        sublane = lax.broadcasted_iota(jnp.int32, (near, 128), 0)
        same = lane // positions == sublane
        at = lane % positions
        ones = jnp.ones((128, HEAD), BF16)

        def part(base):
            here = pl.ds(base, 2 * near)
            there = pl.ds(first + base, 2 * near)
            lines = [pl.ds(base + half * near, near) for half in range(2)]
            seen = [
                same & (at < len_ref[pl.ds((first + base) // near + half, 1), :])
                for half in range(2)
            ]
            table = [jnp.zeros((near, 128), F32) for _ in range(2)]
            for g in range(kv_local):
                at_key, at_value = 2 * g * HEAD, (2 * g + 1) * HEAD
                keys = held[here, :, at_key : at_key + HEAD].reshape(256, HEAD)
                values = held[here, :, at_value : at_value + HEAD].reshape(256, HEAD)
                heads = [slice((g * group + h) * HEAD, (g * group + h + 1) * HEAD) for h in range(group)]
                query = jnp.concatenate([q_ref[there, columns] for columns in heads], axis=0)
                scores = lax.dot_general(
                    query, keys, (((1,), (1,)), ((), ())), preferred_element_type=F32
                ).reshape(group, 2, near, 256)
                results = []
                for half in range(2):
                    own = scores[:, half, :, half * 128 : (half + 1) * 128] * scale
                    own = jnp.where(seen[half][None], own, jnp.float32(-1e30))
                    largest = jnp.max(own, axis=-1, keepdims=True)
                    weight = jnp.exp(own - largest).astype(BF16).reshape(group * near, 128)
                    value = jnp.concatenate([values[half * 128 : (half + 1) * 128], ones], axis=1)
                    mixed = jnp.dot(weight, value, preferred_element_type=F32)
                    total = mixed[:, HEAD:]
                    results.append((mixed[:, :HEAD] / total).reshape(group, near, HEAD))
                    lse = largest + jnp.log(total).reshape(group, near, 128)
                    for h in range(group):
                        table[half] = jnp.where(lane == g * group + h, lse[h], table[half])
                both = jnp.stack(results, axis=1).reshape(group, 2 * near, HEAD).astype(BF16)
                for h, columns in enumerate(heads):
                    out_ref[here, columns] = both[h]
            for half in range(2):
                lse_ref[lines[half], :] = table[half]

        def step(b, carry):
            lines = pl.ds(pl.multiple_of(b * block, block), block)
            pltpu.make_async_copy(kv_ref.at[lines], held.at[lines], sems.at[b]).wait()
            for base in range(0, block, 2 * near):
                part(pl.multiple_of(b * block + base, 2 * near))
            return carry

        lax.fori_loop(0, blocks, step, 0)

    return pl.pallas_call(
        body,
        out_shape=[in_vmem((rows, features), BF16), in_vmem((rows, 128), F32)],
        in_specs=[WHOLE, WHOLE, ANY] + [ANY] * len(after),
        out_specs=[WHOLE, WHOLE],
        scratch_shapes=[
            pltpu.VMEM((rows,) + kv_cache.shape[1:], BF16),
            pltpu.SemaphoreType.DMA((blocks,)),
        ],
        compiler_params=params(20),
        cost_estimate=brief(),
        name="cached",
    )(lengths, queries, in_hbm(kv_cache), *after)


def gather_up(terms, flags, ups, after):
    sizes = [up.shape[0] for up in ups]

    def body(flags_ref, *refs):
        term_refs, up_refs = refs[: len(terms)], refs[len(terms) : len(terms) + len(ups)]
        base_ref, up_ref, sems = refs[-3:]
        copies, at = [], 0
        for n, size in enumerate(sizes):
            copies.append(
                pltpu.make_async_copy(up_refs[n], up_ref.at[pl.ds(at, size)], sems.at[n])
            )
            copies[-1].start()
            at += size
        total = jnp.zeros(base_ref.shape, F32)
        for n, term_ref in enumerate(term_refs):
            total = total + jnp.where(flags_ref[n] == 1, term_ref[...].astype(F32), 0.0)
        base_ref[...] = total
        for copy in copies:
            copy.wait()

    return pl.pallas_call(
        body,
        out_shape=[
            in_vmem(terms[0].shape, F32),
            in_vmem((sum(sizes),) + ups[0].shape[1:], BF16),
        ],
        in_specs=[SCALARS] + [WHOLE] * len(terms) + [ANY] * (len(ups) + len(after)),
        out_specs=[WHOLE, WHOLE],
        scratch_shapes=[pltpu.SemaphoreType.DMA((len(ups),))],
        compiler_params=params(20),
        cost_estimate=brief(),
        name="gather_up",
    )(jnp.stack([jnp.int32(flag) for flag in flags]), *terms, *ups, *after)


def finish(variant_ids, queries, ranges, base, codes_a, codes_b, up, ids):
    rows, features = queries.shape
    width = base.shape[1]
    heads = features // HEAD
    group = features * 2 // width
    chunk = 128
    scale = HEAD ** (-0.5)
    counts = [len(codes_a), len(codes_b)]
    firsts = [0]
    for out1, _ in ranges:
        firsts.append(firsts[-1] + out1.shape[0])

    def body(ids_ref, variant_ref, q_ref, base_ref, up_ref, *refs):
        refs = list(refs)
        done = [(refs.pop(0), refs.pop(0)) for _ in ranges]
        a_refs, b_refs = refs[: counts[0]], refs[counts[0] : counts[0] + counts[1]]
        fresh_ref, attended_ref, fresh_made, attended_made, sems = refs[-5:]
        ones = jnp.ones((2 * HEAD, HEAD), BF16)

        def total(parts, here):
            result = parts[0][here].astype(F32)
            for part in parts[1:]:
                result = result + part[here].astype(F32)
            return result

        stores = []
        for at in range(0, rows, 2 * chunk):
            here = slice(at, at + 2 * chunk)
            variant = variant_ref[here]
            code = jnp.concatenate(
                [total(a_refs, here).astype(BF16), total(b_refs, here).astype(BF16)], axis=1
            )
            masked = [
                jnp.where(variant == ids_ref[entry], code, jnp.zeros_like(code))
                for entry in range(up_ref.shape[0])
            ]
            change = jnp.dot(
                jnp.concatenate(masked, axis=1),
                up_ref[...].reshape(-1, width),
                preferred_element_type=F32,
            )
            fresh = (base_ref[here] + change.astype(BF16).astype(F32)).astype(BF16)
            fresh_made[here] = fresh
        for at in range(0, rows, chunk):
            here = slice(at, at + chunk)
            which = max(n for n in range(len(ranges)) if firsts[n] <= at)
            out1_ref, lse_ref = done[which]
            inner = slice(at - firsts[which], at - firsts[which] + chunk)
            fresh = fresh_made[here]
            keys, values = [], []
            for g in range(width // (2 * HEAD)):
                keys.append(fresh[:, 2 * g * HEAD : (2 * g + 1) * HEAD].astype(F32))
                values.append(fresh[:, (2 * g + 1) * HEAD : (2 * g + 2) * HEAD].astype(F32))
            for h in range(heads):
                columns = slice(h * HEAD, (h + 1) * HEAD)
                product = q_ref[here, columns].astype(F32) * keys[h // group]
                high = product.astype(BF16)
                low = (product - high.astype(F32)).astype(BF16)
                score = jnp.dot(
                    jnp.concatenate([high, low], axis=1), ones, preferred_element_type=F32
                )
                weight = 1.0 / (1.0 + jnp.exp(lse_ref[inner, h : h + 1] - score * scale))
                old = out1_ref[inner, columns].astype(F32)
                moved = old + weight * (values[h // group] - old)
                attended_made[here, columns] = moved.astype(BF16)
            for k, (made, ref) in enumerate(
                ((fresh_made, fresh_ref), (attended_made, attended_ref))
            ):
                lines = pl.ds(at, chunk)
                stores.append(
                    pltpu.make_async_copy(made.at[lines], ref.at[lines], sems.at[k, at // chunk])
                )
                stores[-1].start()
        for store in stores:
            store.wait()

    operands = [variant_ids, queries, base, up]
    for pieces in ranges:
        operands += pieces
    operands += [*codes_a, *codes_b]
    return pl.pallas_call(
        body,
        out_shape=[
            jax.ShapeDtypeStruct((rows, width), BF16),
            jax.ShapeDtypeStruct((rows, features), BF16),
        ],
        in_specs=[SCALARS] + [WHOLE] * len(operands),
        out_specs=[ANY, ANY],
        scratch_shapes=[
            pltpu.VMEM((rows, width), BF16),
            pltpu.VMEM((rows, features), BF16),
            pltpu.SemaphoreType.DMA((2, rows // chunk)),
        ],
        compiler_params=params(20),
        cost_estimate=brief(),
        name="finish",
    )(ids.astype(jnp.int32), *operands)


def all_reduce(value, after=()):
    size = lax.axis_size("tensor")
    bit = 1
    terms = [value]
    while bit < size:
        if len(terms) > 1:
            terms = [added(terms)]
            if after:
                terms = [gate(terms[0], after)]
        terms.append(swap(terms[0], "tensor", bit))
        bit *= 2
    return terms


def reduce_parts(parts):
    size = lax.axis_size("tensor")
    parts = {t: [part] for t, part in parts.items()}
    bit = 1
    while bit < size:
        for t in range(size - 1, 0, -1):
            if t & bit and t & (bit - 1) == 0:
                total = parts[t][0] if len(parts[t]) == 1 else added(parts[t])
                parts[t ^ bit].append(swap(total, "tensor", bit))
        bit *= 2
    return parts[0]


def general(tokens, queries, kv_cache, lengths, variant_ids, base_weight, delta_down, delta_up):
    size, me = lax.axis_size("tensor"), lax.axis_index("tensor")
    width = base_weight.shape[1] // size
    owners = lax.axis_size("adapter")
    variants, _, rank = delta_down.shape
    half = rank // 2
    every = lax.all_gather(delta_down, "adapter", axis=0, tiled=True)
    up = lax.all_gather(delta_up, "adapter", axis=0, tiled=True)
    order = sorted(range(size), key=lambda t: (-(t & 1), -t))
    *parts, token = project(tokens, base_weight, [me ^ t for t in order], width, [])
    base_terms = reduce_parts(dict(zip(order, parts)))
    ids = jnp.arange(owners * variants, dtype=jnp.int32)
    rows_of = [(tokens, variant_ids, None)]
    codes_a, codes_b = [
        all_reduce(codes(rows_of, [every[:, :, at : at + half]], ids, 0, [BF16], [token])[0])
        for at in (0, half)
    ]
    ranges = [cached(queries, kv_cache, lengths, 0, tokens.shape[0], [token])]
    base, up = gather_up(base_terms, [1] * len(base_terms), [up], [])
    return finish(variant_ids, queries, ranges, base, codes_a, codes_b, up, ids)


def paired(tokens, queries, kv_cache, lengths, variant_ids, base_weight, delta_down, delta_up):
    me = lax.axis_index("tensor")
    mine = lax.axis_index("adapter")
    group = lax.axis_index("groups")
    width = base_weight.shape[1] // 4

    rows = tokens.shape[0]
    half = delta_down.shape[2] // 2
    near = swap(tokens, "adapter", 1)
    near_ids = swap(variant_ids, "adapter", 1)
    (first,) = cut(delta_down, [(group, 1, 0)], [])
    from_y = swap(first, "adapter", 2)
    part_3, second, token = project(
        tokens, base_weight, [me ^ 3], width, [first], delta_down, [(0, 2, 1)]
    )
    got_3 = swap(part_3, "tensor", 1)
    far = swap(second, "adapter", 2)
    part_1, part_2, own, token = project(
        tokens, base_weight, [me ^ 1, me ^ 2, me], width, [token], near_adds=[1]
    )
    got_1 = swap(part_1, "tensor", 1)
    from_y = gate(from_y, [token])
    from_x = swap(from_y, "groups", 1)
    start, start_near, near = near_codes(
        tokens,
        variant_ids,
        near,
        near_ids,
        delta_down,
        jnp.stack([2 * mine, 2 * mine + 1]),
        [token, from_y, lengths],
    )
    sum_2 = added([part_2, got_3])
    got_2 = swap(sum_2, "tensor", 2)
    lane = 2 * (mine ^ 2)
    both = [(tokens, variant_ids, start), (near, near_ids, start_near)]
    a, a_near = codes(
        both, [from_y, from_x], jnp.stack([lane + group, lane + 1 - group]), 0, [F32, BF16], [start]
    )
    b, b_near = codes(
        both, [far], jnp.stack([lane, lane + 1]), half, [F32, BF16], [a_near]
    )
    a = added([a, swap(a_near, "adapter", 1)])
    b = added([b, swap(b_near, "adapter", 1)])
    b = gate(b, [got_1, got_2])
    codes_a = all_reduce(a)
    early = cached(queries, kv_cache, lengths, 0, 128, [b])
    codes_b = all_reduce(b, [early[1]])
    late = cached(
        queries, kv_cache, lengths, 128, rows - 128, [early[1], codes_a[0], codes_b[0]]
    )
    ups = [delta_up] + [swap(delta_up, "adapter", bit) for bit in (2, 1, 3)]
    ids = jnp.stack([2 * (mine ^ bit) + j for bit in (0, 2, 1, 3) for j in (0, 1)])
    base, up = gather_up([own, got_1, got_2], [1, 1, 1], ups, [late[1], codes_b[0]])
    return finish(variant_ids, queries, [early, late], base, codes_a, codes_b, up, ids)


def local(tokens, queries, kv_cache, kv_lengths, variant_ids, base_weight, delta_down, delta_up):
    sizes = [lax.axis_size(axis) for axis in ("groups", "adapter", "tensor")]
    plan = paired if sizes == [2, 4, 4] and delta_down.shape[0] == 2 else general
    return tuple(
        plan(
            tokens,
            queries,
            kv_cache,
            jnp.repeat(kv_lengths, kv_cache.shape[1]).reshape(-1, 128),
            variant_ids,
            base_weight,
            delta_down,
            delta_up,
        )
    )


def solution(mesh):
    return jax.shard_map(
        local,
        mesh=mesh,
        in_specs=(
            P(("groups", "adapter"), "tensor"),
            P(("groups", "adapter"), "tensor"),
            P(("groups", "adapter"), None, "tensor"),
            P(("groups", "adapter")),
            P(("groups", "adapter"), None),
            P("tensor", None),
            P("adapter", "tensor", None),
            P("adapter", None, "tensor"),
        ),
        out_specs=(P(("groups", "adapter"), "tensor"), P(("groups", "adapter"), "tensor")),
        check_vma=False,
    )
```
